256 devices in a mesh: dp: 8 (over x, z_hi), ctx: 32 (over y, z_lo, core).
Axes of the slice: x: 4, y: 4, z: 8 (z_hi: 2, z_lo: 4; z = z_hi * 4 + z_lo), core: 2. Of those that a mesh axis runs over, the one named last changes fastest.
Arguments:
- signal: bfloat16 [8, 128, 32768], P('dp', None, 'ctx'), may hold values from -6 to 6
- gate: bfloat16 [8, 128, 32768], P('dp', None, 'ctx'), may hold values from -6 to 6
- filter_param: bfloat16 [128, 32768], P(None, 'ctx'), may hold values from -6 to 6
- cotangent: bfloat16 [8, 128, 32768], P('dp', None, 'ctx'), may hold values from -6 to 6
Outputs:
- gated: bfloat16 [8, 128, 32768], P('dp', None, 'ctx')
- grad_signal: bfloat16 [8, 128, 32768], P('dp', None, 'ctx')
- grad_gate: bfloat16 [8, 128, 32768], P('dp', None, 'ctx')
- grad_filter: bfloat16 [128, 32768], P('dp', 'ctx')
The draws below stay inside these ranges and needn't reach their ends.
All inputs are finite; a program needn't handle non-finite values.
Results may differ from the reference program's by a relative error of at most 0.019.
Values may be sent and summed in bfloat16 or wider, within the bound.
A program may use at most 128 MiB of HBM per device.

```python
import math
import jax
import jax.numpy as jnp
from jax import lax

CH = 128
N1 = 1024
BATCH = 8
SEQ = 32768
NFFT = 65536
N2 = 64


def shard_levels(key, shape, shards, least, high):
    level, own = 1.0, jax.random.fold_in(key, 6)
    for dim, blocks in shards:
        draws = jnp.exp(jax.random.uniform(jax.random.fold_in(own, dim), (blocks,), jnp.float32, least / len(shards), high / len(shards)))
        level = level * jnp.repeat(draws, shape[dim] // blocks).reshape([-1 if axis == dim else 1 for axis in range(len(shape))])
    return level


def gaussian(stream_key, dims, deviation, limit, pieces=(), kind=jnp.bfloat16):
    entries = jax.random.normal(stream_key, dims, jnp.float32) * deviation
    if len(pieces) > 0:
        entries = shard_levels(stream_key, dims, pieces, -0.22, 0.18) * entries
    return jnp.clip(entries, min=-limit, max=limit).astype(kind)


def setup_inputs(seed: int = 0) -> dict:
    seeds = jax.random.split(jax.random.key(seed), 5)
    return {
        "signal": gaussian(seeds[0], (BATCH, CH, SEQ), 1.0, 6.0, ((0, 8), (2, 32))),
        "gate": gaussian(seeds[1], (BATCH, CH, SEQ), 1.0, 6.0, ((0, 8), (2, 32))),
        "filter_param": gaussian(seeds[2], (CH, SEQ), 1.0, 6.0, ((1, 32),)),
        "cotangent": gaussian(seeds[3], (BATCH, CH, SEQ), 1.0, 6.0, ((0, 8), (2, 32))),
    }


def angle_table(row_ids, col_ids, modulus):
    product = (row_ids[:, None] * col_ids[None, :]) % modulus
    return (2.0 * math.pi / modulus) * product.astype(jnp.float32)


def fourier_pair(row_ids, col_ids, modulus):
    angles = angle_table(row_ids, col_ids, modulus)
    return jnp.cos(angles).astype(jnp.bfloat16), jnp.sin(angles).astype(jnp.bfloat16)


def twiddle_pair(row_ids, col_ids, modulus):
    angles = angle_table(row_ids, col_ids, modulus)
    return jnp.cos(angles), jnp.sin(angles)


def reference(signal, gate, filter_param, cotangent):
    half_two = N2 // 2
    every_one = jnp.arange(N1, dtype=jnp.int32)
    every_two = jnp.arange(N2, dtype=jnp.int32)
    cos_one, sin_one = fourier_pair(every_one, every_one, N1)
    cos_two, sin_two = fourier_pair(every_two[:half_two], every_two, N2)
    turn_cos, turn_sin = twiddle_pair(every_two, every_one, NFFT)
    filt_scale = SEQ ** -0.5

    def forward(sequence):
        grid = sequence.reshape(half_two, N1)
        real_a = jnp.dot(cos_two.T, grid, preferred_element_type=jnp.float32)
        imag_a = -jnp.dot(sin_two.T, grid, preferred_element_type=jnp.float32)
        real_b = (real_a * turn_cos + imag_a * turn_sin).astype(jnp.bfloat16)
        imag_b = (imag_a * turn_cos - real_a * turn_sin).astype(jnp.bfloat16)
        real_f = jnp.dot(real_b, cos_one, preferred_element_type=jnp.float32) + jnp.dot(imag_b, sin_one, preferred_element_type=jnp.float32)
        imag_f = jnp.dot(imag_b, cos_one, preferred_element_type=jnp.float32) - jnp.dot(real_b, sin_one, preferred_element_type=jnp.float32)
        return real_f, imag_f

    def inverse(real_z, imag_z, factor):
        real_e = real_z.astype(jnp.bfloat16)
        imag_e = imag_z.astype(jnp.bfloat16)
        real_b = jnp.dot(real_e, cos_one, preferred_element_type=jnp.float32) - jnp.dot(imag_e, sin_one, preferred_element_type=jnp.float32)
        imag_b = jnp.dot(real_e, sin_one, preferred_element_type=jnp.float32) + jnp.dot(imag_e, cos_one, preferred_element_type=jnp.float32)
        real_c = (real_b * turn_cos - imag_b * turn_sin).astype(jnp.bfloat16)
        imag_c = (real_b * turn_sin + imag_b * turn_cos).astype(jnp.bfloat16)
        values = (jnp.dot(cos_two, real_c, preferred_element_type=jnp.float32) - jnp.dot(sin_two, imag_c, preferred_element_type=jnp.float32)) * (1.0 / NFFT)
        return (values * factor).astype(jnp.bfloat16).reshape(SEQ)

    def per_channel(inputs):
        filter_row, signal_rows, gate_rows, grad_rows = inputs
        real_h, imag_h = forward(filter_row)
        real_h = real_h * filt_scale
        imag_h = imag_h * filt_scale

        def per_sequence(running, entry):
            signal_row, gate_row, grad_row = entry
            real_x, imag_x = forward(signal_row)
            conv_seq = inverse(real_h * real_x - imag_h * imag_x, real_h * imag_x + imag_h * real_x, 1.0)
            gated_row = (gate_row.astype(jnp.float32) * conv_seq.astype(jnp.float32)).astype(jnp.bfloat16)
            mid_row = (grad_row.astype(jnp.float32) * gate_row.astype(jnp.float32)).astype(jnp.bfloat16)
            gate_row_grad = (grad_row.astype(jnp.float32) * conv_seq.astype(jnp.float32)).astype(jnp.bfloat16)
            real_g, imag_g = forward(mid_row)
            grad_row_out = inverse(real_h * real_g + imag_h * imag_g, real_h * imag_g - imag_h * real_g, 1.0)
            running = (running[0] + (real_x * real_g + imag_x * imag_g), running[1] + (real_x * imag_g - imag_x * real_g))
            return running, (gated_row, grad_row_out, gate_row_grad)

        empty_sum = jnp.zeros((N2, N1), jnp.float32)
        totals, results = lax.scan(per_sequence, (empty_sum, empty_sum), (signal_rows, gate_rows, grad_rows))
        filter_grad = inverse(totals[0], totals[1], filt_scale)
        return results[0], results[1], results[2], filter_grad

    stacked = lax.map(per_channel, (filter_param, jnp.transpose(signal, (1, 0, 2)), jnp.transpose(gate, (1, 0, 2)), jnp.transpose(cotangent, (1, 0, 2))))
    gated = jnp.transpose(stacked[0], (1, 0, 2))
    grad_signal = jnp.transpose(stacked[1], (1, 0, 2))
    grad_gate = jnp.transpose(stacked[2], (1, 0, 2))
    return (gated, grad_signal, grad_gate, stacked[3])
```

```python
import functools
import math

import jax
import jax.numpy as jnp
import numpy as np
from jax import lax
from jax.experimental import pallas as pl
from jax.experimental.pallas import tpu as pltpu
from jax.sharding import PartitionSpec as P

MESH = pl.DeviceIdType.MESH
F32 = jnp.float32
BF16 = jnp.bfloat16

LANES = 128
ROWS = 256
LENGTH = ROWS * LANES
OWN = 4
UNITS = 8
SCALE = float(LENGTH) ** -1.5


def tables():
    place = np.arange(ROWS, dtype=np.float64)
    lane = np.arange(LANES, dtype=np.float64)
    outer = 2.0 * math.pi / ROWS * (place[:, None] + 0.25) * place[None, :]
    first = np.concatenate([np.cos(outer), -np.sin(outer)], axis=0)
    turn = 2.0 * math.pi / LENGTH * (place[:, None] + 0.25) * lane[None, :]
    inner = 2.0 * math.pi / LANES * lane[:, None] * lane[None, :]
    cos, sin = np.cos(inner), np.sin(inner)
    second = np.concatenate(
        [np.concatenate([cos, -sin], axis=1), np.concatenate([sin, cos], axis=1)], axis=0
    )
    as_b = lambda member: jnp.asarray(member.astype(np.float32)).astype(BF16)
    return (
        as_b(first),
        as_b(first.T),
        as_b(second),
        as_b(second.T),
        jnp.asarray(np.cos(turn).astype(np.float32)),
        jnp.asarray(np.sin(turn).astype(np.float32)),
    )


def kernel(
    ctx_size,
    dp_size,
    signal,
    gate,
    filt,
    cot,
    first,
    first_t,
    second,
    second_t,
    turn_cos,
    turn_sin,
    gated,
    grad_signal,
    grad_gate,
    grad_filter,
    out_buf,
    in_buf,
    stage,
    wide,
    lined,
    mixed,
    spec_h,
    spec_x,
    spec_g,
    send_sem,
    recv_sem,
    ready_sem,
):
    me = lax.axis_index("ctx")
    row = lax.axis_index("dp")
    per_row = ctx_size // dp_size
    SIG, FIL, MID, CNV, GRS, GRF = range(6)

    barrier = pltpu.get_barrier_semaphore()

    def greet_ctx(step, carry):
        peer = lax.rem(me + step, ctx_size)
        pl.semaphore_signal(barrier, inc=1, device_id=(row, peer), device_id_type=MESH)
        return carry

    def greet_dp(step, carry):
        peer = lax.rem(row + step, dp_size)
        pl.semaphore_signal(barrier, inc=1, device_id=(peer, me), device_id_type=MESH)
        return carry

    lax.fori_loop(1, ctx_size, greet_ctx, 0)
    lax.fori_loop(1, dp_size, greet_dp, 0)

    def split_channels(which, block):
        for unit in range(UNITS):
            stage[pl.ds(unit, ctx_size * OWN, stride=UNITS), :] = block(
                pl.ds(unit * LANES, LANES)
            )
        out_buf[which] = stage[...].reshape(ctx_size, OWN * UNITS, LANES).astype(BF16)

    def exchange(which):
        def send(step, carry):
            peer = lax.rem(me + step, ctx_size)
            pltpu.make_async_remote_copy(
                src_ref=out_buf.at[which, peer],
                dst_ref=in_buf.at[which, me],
                send_sem=send_sem.at[which],
                recv_sem=recv_sem.at[which],
                device_id=(row, peer),
                device_id_type=MESH,
            ).start()
            return carry

        lax.fori_loop(1, ctx_size, send, 0)
        in_buf[which, me] = out_buf[which, me]

    def wait_for(sem, which, count):
        part = in_buf.at[which, pl.ds(0, count)]
        pltpu.make_async_copy(part, part, sem.at[which]).wait()

    def transform(which, spec):
        for own in range(OWN):
            part = in_buf[which].astype(F32)[:, own * UNITS : (own + 1) * UNITS, :]
            lined[0:ROWS, own * LANES : (own + 1) * LANES] = part.reshape(ROWS, LANES).astype(BF16)
        wide[...] = jnp.dot(first[...], lined[0:ROWS, :], preferred_element_type=F32)
        for own in range(OWN):
            lanes = slice(own * LANES, (own + 1) * LANES)
            rows = slice(own * ROWS, (own + 1) * ROWS)
            real, imag = wide[0:ROWS, lanes], wide[ROWS : 2 * ROWS, lanes]
            cos, sin = turn_cos[...], turn_sin[...]
            mixed[rows, 0:LANES] = (real * cos + imag * sin).astype(BF16)
            mixed[rows, LANES : 2 * LANES] = (imag * cos - real * sin).astype(BF16)
        spec[...] = jnp.dot(mixed[...], second[...], preferred_element_type=F32)

    def multiply(left, right, conjugate):
        for own in range(OWN):
            rows = slice(own * ROWS, (own + 1) * ROWS)
            left_re, left_im = left[rows, 0:LANES], left[rows, LANES : 2 * LANES]
            right_re, right_im = right[rows, 0:LANES], right[rows, LANES : 2 * LANES]
            if conjugate:
                real = left_re * right_re + left_im * right_im
                imag = left_re * right_im - left_im * right_re
            else:
                real = left_re * right_re - left_im * right_im
                imag = left_re * right_im + left_im * right_re
            mixed[rows, 0:LANES] = real.astype(BF16)
            mixed[rows, LANES : 2 * LANES] = imag.astype(BF16)

    def transform_back(which):
        for own in range(OWN):
            lanes = slice(own * LANES, (own + 1) * LANES)
            rows = slice(own * ROWS, (own + 1) * ROWS)
            both = jnp.dot(mixed[rows, :], second_t[...], preferred_element_type=F32)
            real, imag = both[:, 0:LANES], both[:, LANES : 2 * LANES]
            cos, sin = turn_cos[...], turn_sin[...]
            lined[0:ROWS, lanes] = (real * cos - imag * sin).astype(BF16)
            lined[ROWS : 2 * ROWS, lanes] = (real * sin + imag * cos).astype(BF16)
        values = jnp.dot(first_t[...], lined[...], preferred_element_type=F32) * SCALE
        parts = [
            values[:, own * LANES : (own + 1) * LANES].reshape(ctx_size, UNITS, LANES)
            for own in range(OWN)
        ]
        out_buf[which] = jnp.concatenate(parts, axis=1).astype(BF16)

    def as_f32(ref):
        return lambda lanes: ref[:, lanes].astype(F32)

    split_channels(SIG, as_f32(signal))
    pl.semaphore_wait(barrier, ctx_size - 1 + dp_size - 1)

    def tell_ready(step, carry):
        peer = lax.rem(row + step, dp_size)
        pl.semaphore_signal(ready_sem, inc=1, device_id=(peer, me), device_id_type=MESH)
        return carry

    lax.fori_loop(1, dp_size, tell_ready, 0)

    exchange(SIG)
    split_channels(FIL, as_f32(filt))
    exchange(FIL)
    split_channels(MID, lambda lanes: gate[:, lanes].astype(F32) * cot[:, lanes].astype(F32))
    exchange(MID)

    wait_for(recv_sem, SIG, ctx_size - 1)
    transform(SIG, spec_x)
    wait_for(recv_sem, FIL, ctx_size - 1)
    transform(FIL, spec_h)
    multiply(spec_h, spec_x, False)
    transform_back(CNV)
    exchange(CNV)

    wait_for(recv_sem, MID, ctx_size - 1)
    transform(MID, spec_g)
    multiply(spec_x, spec_g, True)
    transform_back(GRF)
    pl.semaphore_wait(ready_sem, dp_size - 1)
    to_row = me // per_row
    slot = row * per_row + lax.rem(me, per_row)

    def send_filter(step, carry):
        peer = lax.rem(me + step, ctx_size)
        stays = jnp.logical_and(to_row == row, peer == me)

        @pl.when(jnp.logical_not(stays))
        def _():
            pltpu.make_async_remote_copy(
                src_ref=out_buf.at[GRF, peer],
                dst_ref=in_buf.at[GRF, slot],
                send_sem=send_sem.at[GRF],
                recv_sem=recv_sem.at[GRF],
                device_id=(to_row, peer),
                device_id_type=MESH,
            ).start()

        return carry

    lax.fori_loop(0, ctx_size, send_filter, 0)

    @pl.when(to_row == row)
    def _():
        in_buf[GRF, slot] = out_buf[GRF, me]

    multiply(spec_h, spec_g, True)
    transform_back(GRS)
    exchange(GRS)

    wait_for(recv_sem, CNV, ctx_size - 1)
    stage[...] = in_buf[CNV].astype(F32).reshape(ctx_size * OWN * UNITS, LANES)
    for unit in range(UNITS):
        lanes = pl.ds(unit * LANES, LANES)
        conv = stage[pl.ds(unit, ctx_size * OWN, stride=UNITS), :]
        gated[:, lanes] = (gate[:, lanes].astype(F32) * conv).astype(BF16)
        grad_gate[:, lanes] = (cot[:, lanes].astype(F32) * conv).astype(BF16)

    @pl.when(to_row == row)
    def _():
        wait_for(recv_sem, GRF, ctx_size - 1)

    @pl.when(to_row != row)
    def _():
        wait_for(recv_sem, GRF, ctx_size)

    share = per_row * OWN * UNITS
    total = in_buf[GRF, 0:per_row].astype(F32).reshape(share, LANES)
    for other in range(1, dp_size):
        part = in_buf[GRF, other * per_row : (other + 1) * per_row]
        total = total + part.astype(F32).reshape(share, LANES)
    stage[0:share, :] = total
    for unit in range(UNITS):
        lanes = pl.ds(unit * LANES, LANES)
        grad_filter[:, lanes] = stage[pl.ds(unit, per_row * OWN, stride=UNITS), :].astype(BF16)

    wait_for(recv_sem, GRS, ctx_size - 1)
    stage[...] = in_buf[GRS].astype(F32).reshape(ctx_size * OWN * UNITS, LANES)
    for unit in range(UNITS):
        lanes = pl.ds(unit * LANES, LANES)
        grad_signal[:, lanes] = stage[pl.ds(unit, ctx_size * OWN, stride=UNITS), :].astype(BF16)

    for which in (SIG, FIL, MID, CNV, GRS):
        wait_for(send_sem, which, ctx_size - 1)

    @pl.when(to_row == row)
    def _():
        wait_for(send_sem, GRF, ctx_size - 1)

    @pl.when(to_row != row)
    def _():
        wait_for(send_sem, GRF, ctx_size)


def per_device(signal, gate, filter_param, cotangent):
    ctx_size = lax.axis_size("ctx")
    dp_size = lax.axis_size("dp")
    channels, length = filter_param.shape
    block = jax.ShapeDtypeStruct((channels, length), BF16)
    share = jax.ShapeDtypeStruct((channels // dp_size, length), BF16)
    whole = pl.BlockSpec(memory_space=pltpu.VMEM)
    messages = (6, ctx_size, OWN * UNITS, LANES)
    outs = pl.pallas_call(
        functools.partial(kernel, ctx_size, dp_size),
        out_shape=(block, block, block, share),
        in_specs=[whole] * 10,
        out_specs=(whole,) * 4,
        scratch_shapes=[
            pltpu.VMEM(messages, BF16),
            pltpu.VMEM(messages, BF16),
            pltpu.VMEM((ctx_size * OWN * UNITS, LANES), F32),
            pltpu.VMEM((2 * ROWS, OWN * LANES), F32),
            pltpu.VMEM((2 * ROWS, OWN * LANES), BF16),
            pltpu.VMEM((OWN * ROWS, 2 * LANES), BF16),
            pltpu.VMEM((OWN * ROWS, 2 * LANES), F32),
            pltpu.VMEM((OWN * ROWS, 2 * LANES), F32),
            pltpu.VMEM((OWN * ROWS, 2 * LANES), F32),
            pltpu.SemaphoreType.DMA((6,)),
            pltpu.SemaphoreType.DMA((6,)),
            pltpu.SemaphoreType.REGULAR,
        ],
        compiler_params=pltpu.CompilerParams(
            collective_id=0, has_side_effects=True, vmem_limit_bytes=48 * 1024 * 1024
        ),
    )(
        signal.reshape(channels, length),
        gate.reshape(channels, length),
        filter_param,
        cotangent.reshape(channels, length),
        *tables(),
    )
    return (outs[0][None], outs[1][None], outs[2][None], outs[3])


def solution(mesh):
    in_specs = (P("dp", None, "ctx"), P("dp", None, "ctx"), P(None, "ctx"), P("dp", None, "ctx"))
    out_specs = (P("dp", None, "ctx"), P("dp", None, "ctx"), P("dp", None, "ctx"), P("dp", "ctx"))
    return jax.shard_map(
        per_device, mesh=mesh, in_specs=in_specs, out_specs=out_specs, check_vma=False
    )
```

```python
import functools
import math

import jax
import jax.numpy as jnp
import numpy as np
from jax import lax
from jax.experimental import pallas as pl
from jax.experimental.pallas import tpu as pltpu
from jax.sharding import PartitionSpec as P

MESH = pl.DeviceIdType.MESH
F32 = jnp.float32
BF16 = jnp.bfloat16

LANES = 128
ROWS = 256
LENGTH = ROWS * LANES
OWN = 4
UNITS = 8
SCALE = float(LENGTH) ** -1.5


def tables():
    place = np.arange(ROWS, dtype=np.float64)
    lane = np.arange(LANES, dtype=np.float64)
    outer = 2.0 * math.pi / ROWS * (place[:, None] + 0.25) * place[None, :]
    first = np.concatenate([np.cos(outer), -np.sin(outer)], axis=0)
    turn = 2.0 * math.pi / LENGTH * (place[:, None] + 0.25) * lane[None, :]
    inner = 2.0 * math.pi / LANES * lane[:, None] * lane[None, :]
    cos, sin = np.cos(inner), np.sin(inner)
    second = np.concatenate(
        [np.concatenate([cos, -sin], axis=1), np.concatenate([sin, cos], axis=1)], axis=0
    )
    as_b = lambda member: jnp.asarray(member.astype(np.float32)).astype(BF16)
    return (
        as_b(first),
        as_b(first.T),
        as_b(second),
        as_b(second.T),
        jnp.asarray(np.cos(turn).astype(np.float32)),
        jnp.asarray(np.sin(turn).astype(np.float32)),
    )


def kernel(
    ctx_size,
    dp_size,
    signal_hbm,
    gate_hbm,
    filt_hbm,
    cot_hbm,
    first_hbm,
    first_t_hbm,
    second_hbm,
    second_t_hbm,
    turn_cos_hbm,
    turn_sin_hbm,
    gated,
    grad_signal,
    grad_gate,
    grad_filter,
    signal,
    gate,
    filt,
    cot,
    first,
    first_t,
    second,
    second_t,
    turn_cos,
    turn_sin,
    out_buf,
    in_buf,
    in_filt,
    in_part,
    out_sum,
    in_sum,
    stage,
    wide,
    lined,
    mixed,
    spec_h,
    spec_x,
    spec_g,
    send_sem,
    recv_sem,
    load_sem,
):
    me = lax.axis_index("ctx")
    row = lax.axis_index("dp")
    per_row = ctx_size // dp_size
    lanes_x = dp_size // 2
    my_x, my_z = row // 2, lax.rem(row, 2)
    share = ctx_size // lanes_x
    my_y, my_low = me // share, lax.rem(me, share) // 2
    SIG, MID, CNV, GRS, FIL, GRF = range(6)
    FIL_X, GRF_X = 6, 7

    loads = [
        pltpu.make_async_copy(source, target, load_sem.at[index])
        for index, (source, target) in enumerate(
            (
                (filt_hbm, filt),
                (signal_hbm, signal),
                (gate_hbm, gate),
                (cot_hbm, cot),
                (first_hbm, first),
                (turn_cos_hbm, turn_cos),
                (turn_sin_hbm, turn_sin),
                (second_hbm, second),
                (second_t_hbm, second_t),
                (first_t_hbm, first_t),
            )
        )
    ]

    barrier = pltpu.get_barrier_semaphore()

    def greet_ctx(step, carry):
        peer = lax.rem(me + step, ctx_size)
        pl.semaphore_signal(barrier, inc=1, device_id=(row, peer), device_id_type=MESH)
        return carry

    lax.fori_loop(1, ctx_size, greet_ctx, 0)
    for step in range(1, lanes_x):
        peer = lax.rem(my_x + step, lanes_x) * 2 + my_z
        pl.semaphore_signal(barrier, inc=1, device_id=(peer, me), device_id_type=MESH)
    other = my_x * 2 + 1 - my_z
    pl.semaphore_signal(barrier, inc=1, device_id=(other, me), device_id_type=MESH)

    for copy in loads:
        copy.start()

    def split_channels(which, block):
        for unit in range(UNITS):
            stage[pl.ds(unit, ctx_size * OWN, stride=UNITS), :] = block(
                pl.ds(unit * LANES, LANES)
            )
        out_buf[which] = stage[...].reshape(ctx_size, OWN * UNITS, LANES).astype(BF16)

    def remote(source, target, sem, device):
        pltpu.make_async_remote_copy(
            src_ref=source,
            dst_ref=target,
            send_sem=send_sem.at[sem],
            recv_sem=recv_sem.at[sem],
            device_id=device,
            device_id_type=MESH,
        ).start()

    def exchange(which):
        def send(step, carry):
            peer = lax.rem(me + step, ctx_size)
            remote(out_buf.at[which, peer], in_buf.at[which, me], which, (row, peer))
            return carry

        lax.fori_loop(1, ctx_size, send, 0)
        in_buf[which, me] = out_buf[which, me]

    def wait_for(sem, which, count):
        part = in_buf.at[0, pl.ds(0, count)]
        pltpu.make_async_copy(part, part, sem.at[which]).wait()

    def wait_either(sem, which, count, less):
        @pl.when(less)
        def _():
            wait_for(sem, which, count - 1)

        @pl.when(jnp.logical_not(less))
        def _():
            wait_for(sem, which, count)

    def line_up(part, block, blocks):
        part = part.astype(F32)
        for own in range(OWN):
            rows = part[:, own * UNITS : (own + 1) * UNITS, :].reshape(blocks * UNITS, LANES)
            lined[
                block * UNITS : (block + blocks) * UNITS, own * LANES : (own + 1) * LANES
            ] = rows.astype(BF16)

    def transform(spec):
        wide[...] = jnp.dot(first[...], lined[0:ROWS, :], preferred_element_type=F32)
        for own in range(OWN):
            lanes = slice(own * LANES, (own + 1) * LANES)
            rows = slice(own * ROWS, (own + 1) * ROWS)
            real, imag = wide[0:ROWS, lanes], wide[ROWS : 2 * ROWS, lanes]
            cos, sin = turn_cos[...], turn_sin[...]
            mixed[rows, 0:LANES] = (real * cos + imag * sin).astype(BF16)
            mixed[rows, LANES : 2 * LANES] = (imag * cos - real * sin).astype(BF16)
        spec[...] = jnp.dot(mixed[...], second[...], preferred_element_type=F32)

    def multiply(left, right, conjugate):
        for own in range(OWN):
            rows = slice(own * ROWS, (own + 1) * ROWS)
            left_re, left_im = left[rows, 0:LANES], left[rows, LANES : 2 * LANES]
            right_re, right_im = right[rows, 0:LANES], right[rows, LANES : 2 * LANES]
            if conjugate:
                real = left_re * right_re + left_im * right_im
                imag = left_re * right_im - left_im * right_re
            else:
                real = left_re * right_re - left_im * right_im
                imag = left_re * right_im + left_im * right_re
            mixed[rows, 0:LANES] = real.astype(BF16)
            mixed[rows, LANES : 2 * LANES] = imag.astype(BF16)

    def transform_back(which):
        for own in range(OWN):
            lanes = slice(own * LANES, (own + 1) * LANES)
            rows = slice(own * ROWS, (own + 1) * ROWS)
            both = jnp.dot(mixed[rows, :], second_t[...], preferred_element_type=F32)
            real, imag = both[:, 0:LANES], both[:, LANES : 2 * LANES]
            cos, sin = turn_cos[...], turn_sin[...]
            lined[0:ROWS, lanes] = (real * cos - imag * sin).astype(BF16)
            lined[ROWS : 2 * ROWS, lanes] = (real * sin + imag * cos).astype(BF16)
        values = jnp.dot(first_t[...], lined[...], preferred_element_type=F32) * SCALE
        parts = [
            values[:, own * LANES : (own + 1) * LANES].reshape(ctx_size, UNITS, LANES)
            for own in range(OWN)
        ]
        out_buf[which] = jnp.concatenate(parts, axis=1).astype(BF16)

    fetches = lax.rem(my_y + my_low, lanes_x) == my_x
    filt_slot = 2 * my_y + lax.rem(me, 2)

    loads[0].wait()

    @pl.when(fetches)
    def _():
        split_channels(FIL, lambda lanes: filt[:, lanes].astype(F32))

    loads[1].wait()
    split_channels(SIG, lambda lanes: signal[:, lanes].astype(F32))
    pl.semaphore_wait(barrier, ctx_size - 1 + lanes_x)

    @pl.when(fetches)
    def _():
        def send(step, carry):
            peer = lax.rem(me + step, ctx_size)
            remote(out_buf.at[FIL, peer], in_filt.at[my_x, filt_slot], FIL, (row, peer))
            return carry

        lax.fori_loop(1, ctx_size, send, 0)
        in_filt[my_x, filt_slot] = out_buf[FIL, me]

    exchange(SIG)
    loads[2].wait()
    loads[3].wait()
    split_channels(MID, lambda lanes: gate[:, lanes].astype(F32) * cot[:, lanes].astype(F32))
    wait_either(recv_sem, FIL, share, fetches)
    for step in range(1, lanes_x):
        peer = lax.rem(my_x + step, lanes_x) * 2 + my_z
        remote(in_filt.at[my_x], in_filt.at[my_x], FIL_X, (peer, me))
    exchange(MID)

    for copy in loads[4:]:
        copy.wait()
    wait_for(recv_sem, SIG, ctx_size - 1)
    line_up(in_buf[SIG], 0, ctx_size)
    transform(spec_x)
    wait_for(recv_sem, FIL_X, share * (lanes_x - 1))
    for pair in range(ctx_size // 2):
        part_y, part_low = pair // (share // 2), pair % (share // 2)
        group = (part_y + part_low) % lanes_x
        line_up(in_filt[group, 2 * part_y : 2 * part_y + 2], 2 * pair, 2)
    transform(spec_h)
    multiply(spec_h, spec_x, False)
    transform_back(CNV)
    exchange(CNV)

    wait_for(recv_sem, MID, ctx_size - 1)
    line_up(in_buf[MID], 0, ctx_size)
    transform(spec_g)
    multiply(spec_x, spec_g, True)
    transform_back(GRF)
    for step in range(1, lanes_x):
        peer = lax.rem(my_x + step, lanes_x)
        blocks = out_buf.at[GRF, pl.ds(peer * share, share)]
        remote(blocks, in_part.at[my_x], GRF_X, (peer * 2 + my_z, me))
    in_part[my_x] = out_buf[GRF, pl.ds(my_x * share, share)]

    multiply(spec_h, spec_g, True)
    transform_back(GRS)
    exchange(GRS)

    wait_for(recv_sem, GRF_X, share * (lanes_x - 1))
    total = in_part[0].astype(F32)
    for part in range(1, lanes_x):
        total = total + in_part[part].astype(F32)
    out_sum[...] = total.astype(BF16)
    to_row = me // per_row
    slot = my_z * per_row + lax.rem(me, per_row)
    stays = jnp.logical_and(to_row == row, me // share == my_x)

    def send_sum(block, carry):
        peer = my_x * share + block
        leaves = jnp.logical_or(to_row != row, peer != me)

        @pl.when(leaves)
        def _():
            remote(out_sum.at[block], in_sum.at[slot], GRF, (to_row, peer))

        return carry

    lax.fori_loop(0, share, send_sum, 0)

    @pl.when(stays)
    def _():
        in_sum[slot] = out_sum[lax.rem(me, share)]

    wait_for(recv_sem, CNV, ctx_size - 1)
    stage[...] = in_buf[CNV].astype(F32).reshape(ctx_size * OWN * UNITS, LANES)
    for unit in range(UNITS):
        lanes = pl.ds(unit * LANES, LANES)
        conv = stage[pl.ds(unit, ctx_size * OWN, stride=UNITS), :]
        gated[:, lanes] = (gate[:, lanes].astype(F32) * conv).astype(BF16)
        grad_gate[:, lanes] = (cot[:, lanes].astype(F32) * conv).astype(BF16)

    wait_either(recv_sem, GRF, 2 * per_row, stays)
    total = in_sum[0:per_row].astype(F32) + in_sum[per_row : 2 * per_row].astype(F32)
    stage[0 : per_row * OWN * UNITS, :] = total.reshape(per_row * OWN * UNITS, LANES)
    for unit in range(UNITS):
        lanes = pl.ds(unit * LANES, LANES)
        grad_filter[:, lanes] = stage[pl.ds(unit, per_row * OWN, stride=UNITS), :].astype(BF16)

    wait_for(recv_sem, GRS, ctx_size - 1)
    stage[...] = in_buf[GRS].astype(F32).reshape(ctx_size * OWN * UNITS, LANES)
    for unit in range(UNITS):
        lanes = pl.ds(unit * LANES, LANES)
        grad_signal[:, lanes] = stage[pl.ds(unit, ctx_size * OWN, stride=UNITS), :].astype(BF16)

    for which in (SIG, MID, CNV, GRS):
        wait_for(send_sem, which, ctx_size - 1)
    for which in (FIL_X, GRF_X):
        wait_for(send_sem, which, share * (lanes_x - 1))
    wait_either(send_sem, GRF, share, stays)

    @pl.when(fetches)
    def _():
        wait_for(send_sem, FIL, ctx_size - 1)


def hand_on(*refs):
    sources, targets, sem = refs[0:4], refs[4:8], refs[8]
    copies = [
        pltpu.make_async_copy(source, target, sem.at[index])
        for index, (source, target) in enumerate(zip(sources, targets))
    ]
    for copy in copies:
        copy.start()
    for copy in copies:
        copy.wait()


def per_device(signal, gate, filter_param, cotangent):
    ctx_size = lax.axis_size("ctx")
    dp_size = lax.axis_size("dp")
    channels, length = filter_param.shape
    lanes_x = dp_size // 2
    share = ctx_size // lanes_x
    block = (channels, length)
    part = (channels // dp_size, length)
    outer = pl.BlockSpec(memory_space=pltpu.HBM)
    inner = pl.BlockSpec(memory_space=pltpu.VMEM)
    message = (OWN * UNITS, LANES)
    spectrum = pltpu.VMEM((OWN * ROWS, 2 * LANES), F32)
    outs = pl.pallas_call(
        functools.partial(kernel, ctx_size, dp_size),
        out_shape=tuple(pltpu.VMEM(shape, BF16) for shape in (block, block, block, part)),
        in_specs=[outer] * 10,
        out_specs=(inner,) * 4,
        scratch_shapes=[
            pltpu.VMEM(block, BF16),
            pltpu.VMEM(block, BF16),
            pltpu.VMEM(block, BF16),
            pltpu.VMEM(block, BF16),
            pltpu.VMEM((2 * ROWS, ROWS), BF16),
            pltpu.VMEM((ROWS, 2 * ROWS), BF16),
            pltpu.VMEM((2 * LANES, 2 * LANES), BF16),
            pltpu.VMEM((2 * LANES, 2 * LANES), BF16),
            pltpu.VMEM((ROWS, LANES), F32),
            pltpu.VMEM((ROWS, LANES), F32),
            pltpu.VMEM((6, ctx_size) + message, BF16),
            pltpu.VMEM((4, ctx_size) + message, BF16),
            pltpu.VMEM((lanes_x, share) + message, BF16),
            pltpu.VMEM((lanes_x, share) + message, BF16),
            pltpu.VMEM((share,) + message, BF16),
            pltpu.VMEM((2 * ctx_size // dp_size,) + message, BF16),
            pltpu.VMEM((ctx_size * OWN * UNITS, LANES), F32),
            pltpu.VMEM((2 * ROWS, OWN * LANES), F32),
            pltpu.VMEM((2 * ROWS, OWN * LANES), BF16),
            pltpu.VMEM((OWN * ROWS, 2 * LANES), BF16),
            spectrum,
            spectrum,
            spectrum,
            pltpu.SemaphoreType.DMA((8,)),
            pltpu.SemaphoreType.DMA((8,)),
            pltpu.SemaphoreType.DMA((10,)),
        ],
        compiler_params=pltpu.CompilerParams(
            collective_id=0, has_side_effects=True, vmem_limit_bytes=60 * 1024 * 1024
        ),
    )(
        signal.reshape(block),
        gate.reshape(block),
        filter_param,
        cotangent.reshape(block),
        *tables(),
    )
    outs = pl.pallas_call(
        hand_on,
        out_shape=tuple(jax.ShapeDtypeStruct(shape, BF16) for shape in (block, block, block, part)),
        in_specs=[inner] * 4,
        out_specs=(outer,) * 4,
        scratch_shapes=[pltpu.SemaphoreType.DMA((4,))],
    )(*outs)
    return (outs[0][None], outs[1][None], outs[2][None], outs[3])


def solution(mesh):
    in_specs = (P("dp", None, "ctx"), P("dp", None, "ctx"), P(None, "ctx"), P("dp", None, "ctx"))
    out_specs = (P("dp", None, "ctx"), P("dp", None, "ctx"), P("dp", None, "ctx"), P("dp", "ctx"))
    return jax.shard_map(
        per_device, mesh=mesh, in_specs=in_specs, out_specs=out_specs, check_vma=False
    )
```

```python
import functools
import math

import jax
import jax.numpy as jnp
import numpy as np
from jax import lax
from jax.experimental import pallas as pl
from jax.experimental.pallas import tpu as pltpu
from jax.sharding import PartitionSpec as P

MESH = pl.DeviceIdType.MESH
F32 = jnp.float32
BF16 = jnp.bfloat16

LANES = 128
ROWS = 256
LENGTH = ROWS * LANES
OWN = 4
UNITS = 8
SCALE = float(LENGTH) ** -1.5


def tables():
    place = np.arange(ROWS, dtype=np.float64)
    lane = np.arange(LANES, dtype=np.float64)
    outer = 2.0 * math.pi / ROWS * (place[:, None] + 0.25) * place[None, :]
    first = np.concatenate([np.cos(outer), -np.sin(outer)], axis=0)
    turn = 2.0 * math.pi / LENGTH * (place[:, None] + 0.25) * lane[None, :]
    inner = 2.0 * math.pi / LANES * lane[:, None] * lane[None, :]
    cos, sin = np.cos(inner), np.sin(inner)
    second = np.concatenate(
        [np.concatenate([cos, -sin], axis=1), np.concatenate([sin, cos], axis=1)], axis=0
    )
    as_b = lambda member: jnp.asarray(member.astype(np.float32)).astype(BF16)
    return (
        as_b(first),
        as_b(first.T),
        as_b(second),
        as_b(second.T),
        jnp.asarray(np.cos(turn).astype(np.float32)),
        jnp.asarray(np.sin(turn).astype(np.float32)),
    )


def kernel(
    ctx_size,
    dp_size,
    signal_hbm,
    gate_hbm,
    filt_hbm,
    cot_hbm,
    first_hbm,
    first_t_hbm,
    second_hbm,
    second_t_hbm,
    turn_cos_hbm,
    turn_sin_hbm,
    gated,
    grad_signal,
    grad_gate,
    grad_filter,
    signal,
    gate,
    filt,
    cot,
    first,
    first_t,
    second,
    second_t,
    turn_cos,
    turn_sin,
    out_buf,
    in_buf,
    in_filt,
    in_part,
    out_sum,
    in_sum,
    stage,
    wide,
    lined,
    mixed,
    spec_h,
    spec_x,
    spec_g,
    send_sem,
    recv_sem,
    load_sem,
):
    me = lax.axis_index("ctx")
    row = lax.axis_index("dp")
    per_row = ctx_size // dp_size
    lanes_x = dp_size // 2
    my_x, my_z = row // 2, lax.rem(row, 2)
    share = ctx_size // lanes_x
    my_y, my_low = me // share, lax.rem(me, share) // 2
    SIG, MID, CNV, GRS, FIL, GRF = range(6)
    FIL_X, GRF_X = 6, 7

    loads = [
        pltpu.make_async_copy(source, target, load_sem.at[index])
        for index, (source, target) in enumerate(
            (
                (filt_hbm, filt),
                (signal_hbm, signal),
                (gate_hbm, gate),
                (cot_hbm, cot),
                (first_hbm, first),
                (turn_cos_hbm, turn_cos),
                (turn_sin_hbm, turn_sin),
                (second_hbm, second),
                (second_t_hbm, second_t),
                (first_t_hbm, first_t),
            )
        )
    ]

    barrier = pltpu.get_barrier_semaphore()

    def greet_ctx(step, carry):
        peer = lax.rem(me + step, ctx_size)
        pl.semaphore_signal(barrier, inc=1, device_id=(row, peer), device_id_type=MESH)
        return carry

    lax.fori_loop(1, ctx_size, greet_ctx, 0)
    for step in range(1, lanes_x):
        peer = lax.rem(my_x + step, lanes_x) * 2 + my_z
        pl.semaphore_signal(barrier, inc=1, device_id=(peer, me), device_id_type=MESH)
    other = my_x * 2 + 1 - my_z
    pl.semaphore_signal(barrier, inc=1, device_id=(other, me), device_id_type=MESH)

    for copy in loads:
        copy.start()

    def split_channels(which, block):
        for unit in range(UNITS):
            stage[pl.ds(unit, ctx_size * OWN, stride=UNITS), :] = block(
                pl.ds(unit * LANES, LANES)
            )
        out_buf[which] = stage[...].reshape(ctx_size, OWN * UNITS, LANES).astype(BF16)

    def remote(source, target, sem, device):
        pltpu.make_async_remote_copy(
            src_ref=source,
            dst_ref=target,
            send_sem=send_sem.at[sem],
            recv_sem=recv_sem.at[sem],
            device_id=device,
            device_id_type=MESH,
        ).start()

    def exchange(which):
        def send(step, carry):
            peer = lax.rem(me + step, ctx_size)
            remote(out_buf.at[which, peer], in_buf.at[which, me], which, (row, peer))
            return carry

        lax.fori_loop(1, ctx_size, send, 0)
        in_buf[which, me] = out_buf[which, me]

    def wait_for(sem, which, count):
        part = in_buf.at[0, pl.ds(0, count)]
        pltpu.make_async_copy(part, part, sem.at[which]).wait()

    def wait_either(sem, which, count, less):
        @pl.when(less)
        def _():
            wait_for(sem, which, count - 1)

        @pl.when(jnp.logical_not(less))
        def _():
            wait_for(sem, which, count)

    def line_up(part, block, blocks):
        part = part.astype(F32)
        for own in range(OWN):
            rows = part[:, own * UNITS : (own + 1) * UNITS, :].reshape(blocks * UNITS, LANES)
            lined[
                block * UNITS : (block + blocks) * UNITS, own * LANES : (own + 1) * LANES
            ] = rows.astype(BF16)

    def transform(spec):
        wide[...] = jnp.dot(first[...], lined[0:ROWS, :], preferred_element_type=F32)
        for own in range(OWN):
            lanes = slice(own * LANES, (own + 1) * LANES)
            rows = slice(own * ROWS, (own + 1) * ROWS)
            real, imag = wide[0:ROWS, lanes], wide[ROWS : 2 * ROWS, lanes]
            cos, sin = turn_cos[...], turn_sin[...]
            mixed[rows, 0:LANES] = (real * cos + imag * sin).astype(BF16)
            mixed[rows, LANES : 2 * LANES] = (imag * cos - real * sin).astype(BF16)
        spec[...] = jnp.dot(mixed[...], second[...], preferred_element_type=F32)

    def multiply(left, right, conjugate):
        for own in range(OWN):
            rows = slice(own * ROWS, (own + 1) * ROWS)
            left_re, left_im = left[rows, 0:LANES], left[rows, LANES : 2 * LANES]
            right_re, right_im = right[rows, 0:LANES], right[rows, LANES : 2 * LANES]
            if conjugate:
                real = left_re * right_re + left_im * right_im
                imag = left_re * right_im - left_im * right_re
            else:
                real = left_re * right_re - left_im * right_im
                imag = left_re * right_im + left_im * right_re
            mixed[rows, 0:LANES] = real.astype(BF16)
            mixed[rows, LANES : 2 * LANES] = imag.astype(BF16)

    def transform_back(which):
        for own in range(OWN):
            lanes = slice(own * LANES, (own + 1) * LANES)
            rows = slice(own * ROWS, (own + 1) * ROWS)
            both = jnp.dot(mixed[rows, :], second_t[...], preferred_element_type=F32)
            real, imag = both[:, 0:LANES], both[:, LANES : 2 * LANES]
            cos, sin = turn_cos[...], turn_sin[...]
            lined[0:ROWS, lanes] = (real * cos - imag * sin).astype(BF16)
            lined[ROWS : 2 * ROWS, lanes] = (real * sin + imag * cos).astype(BF16)
        values = jnp.dot(first_t[...], lined[...], preferred_element_type=F32) * SCALE
        parts = [
            values[:, own * LANES : (own + 1) * LANES].reshape(ctx_size, UNITS, LANES)
            for own in range(OWN)
        ]
        out_buf[which] = jnp.concatenate(parts, axis=1).astype(BF16)

    fetches = lax.rem(my_y + my_low, lanes_x) == my_x
    filt_slot = 2 * my_y + lax.rem(me, 2)

    loads[0].wait()

    @pl.when(fetches)
    def _():
        split_channels(FIL, lambda lanes: filt[:, lanes].astype(F32))

    loads[1].wait()
    split_channels(SIG, lambda lanes: signal[:, lanes].astype(F32))
    pl.semaphore_wait(barrier, ctx_size - 1 + lanes_x)

    @pl.when(fetches)
    def _():
        def send(step, carry):
            peer = lax.rem(me + step, ctx_size)
            remote(out_buf.at[FIL, peer], in_filt.at[my_x, filt_slot], FIL, (row, peer))
            return carry

        lax.fori_loop(1, ctx_size, send, 0)
        in_filt[my_x, filt_slot] = out_buf[FIL, me]

    exchange(SIG)
    loads[2].wait()
    loads[3].wait()
    split_channels(MID, lambda lanes: gate[:, lanes].astype(F32) * cot[:, lanes].astype(F32))
    wait_either(recv_sem, FIL, share, fetches)
    for step in range(1, lanes_x):
        peer = lax.rem(my_x + step, lanes_x) * 2 + my_z
        remote(in_filt.at[my_x], in_filt.at[my_x], FIL_X, (peer, me))
    exchange(MID)

    for copy in loads[4:]:
        copy.wait()
    wait_for(recv_sem, SIG, ctx_size - 1)
    line_up(in_buf[SIG], 0, ctx_size)
    transform(spec_x)
    wait_for(recv_sem, FIL_X, share * (lanes_x - 1))
    for pair in range(ctx_size // 2):
        part_y, part_low = pair // (share // 2), pair % (share // 2)
        group = (part_y + part_low) % lanes_x
        line_up(in_filt[group, 2 * part_y : 2 * part_y + 2], 2 * pair, 2)
    transform(spec_h)
    multiply(spec_h, spec_x, False)
    transform_back(CNV)
    exchange(CNV)

    wait_for(recv_sem, MID, ctx_size - 1)
    line_up(in_buf[MID], 0, ctx_size)
    transform(spec_g)
    multiply(spec_x, spec_g, True)
    transform_back(GRF)
    for step in range(1, lanes_x):
        peer = lax.rem(my_x + step, lanes_x)
        blocks = out_buf.at[GRF, pl.ds(peer * share, share)]
        remote(blocks, in_part.at[my_x], GRF_X, (peer * 2 + my_z, me))
    in_part[my_x] = out_buf[GRF, pl.ds(my_x * share, share)]

    multiply(spec_h, spec_g, True)
    transform_back(GRS)
    exchange(GRS)

    wait_for(recv_sem, GRF_X, share * (lanes_x - 1))
    total = in_part[0].astype(F32)
    for part in range(1, lanes_x):
        total = total + in_part[part].astype(F32)
    out_sum[...] = total.astype(BF16)
    to_row = me // per_row
    slot = my_z * per_row + lax.rem(me, per_row)
    stays = jnp.logical_and(to_row == row, me // share == my_x)

    def send_sum(block, carry):
        peer = my_x * share + block
        leaves = jnp.logical_or(to_row != row, peer != me)

        @pl.when(leaves)
        def _():
            remote(out_sum.at[block], in_sum.at[slot], GRF, (to_row, peer))

        return carry

    lax.fori_loop(0, share, send_sum, 0)

    @pl.when(stays)
    def _():
        in_sum[slot] = out_sum[lax.rem(me, share)]

    wait_for(recv_sem, CNV, ctx_size - 1)
    stage[...] = in_buf[CNV].astype(F32).reshape(ctx_size * OWN * UNITS, LANES)
    for unit in range(UNITS):
        lanes = pl.ds(unit * LANES, LANES)
        conv = stage[pl.ds(unit, ctx_size * OWN, stride=UNITS), :]
        gated[:, lanes] = (gate[:, lanes].astype(F32) * conv).astype(BF16)
        grad_gate[:, lanes] = (cot[:, lanes].astype(F32) * conv).astype(BF16)

    wait_either(recv_sem, GRF, 2 * per_row, stays)
    total = in_sum[0:per_row].astype(F32) + in_sum[per_row : 2 * per_row].astype(F32)
    stage[0 : per_row * OWN * UNITS, :] = total.reshape(per_row * OWN * UNITS, LANES)
    for unit in range(UNITS):
        lanes = pl.ds(unit * LANES, LANES)
        grad_filter[:, lanes] = stage[pl.ds(unit, per_row * OWN, stride=UNITS), :].astype(BF16)

    wait_for(recv_sem, GRS, ctx_size - 1)
    stage[...] = in_buf[GRS].astype(F32).reshape(ctx_size * OWN * UNITS, LANES)
    for unit in range(UNITS):
        lanes = pl.ds(unit * LANES, LANES)
        grad_signal[:, lanes] = stage[pl.ds(unit, ctx_size * OWN, stride=UNITS), :].astype(BF16)

    for which in (SIG, MID, CNV, GRS):
        wait_for(send_sem, which, ctx_size - 1)
    for which in (FIL_X, GRF_X):
        wait_for(send_sem, which, share * (lanes_x - 1))
    wait_either(send_sem, GRF, share, stays)

    @pl.when(fetches)
    def _():
        wait_for(send_sem, FIL, ctx_size - 1)


def hand_on(*refs):
    sources, targets, sem = refs[0:4], refs[4:8], refs[8]
    copies = [
        pltpu.make_async_copy(source, target, sem.at[index])
        for index, (source, target) in enumerate(zip(sources, targets))
    ]
    for copy in copies:
        copy.start()
    for copy in copies:
        copy.wait()


def per_device(signal, gate, filter_param, cotangent):
    ctx_size = lax.axis_size("ctx")
    dp_size = lax.axis_size("dp")
    channels, length = filter_param.shape
    lanes_x = dp_size // 2
    share = ctx_size // lanes_x
    block = (channels, length)
    part = (channels // dp_size, length)
    outer = pl.BlockSpec(memory_space=pltpu.HBM)
    inner = pl.BlockSpec(memory_space=pltpu.VMEM)
    message = (OWN * UNITS, LANES)
    spectrum = pltpu.VMEM((OWN * ROWS, 2 * LANES), F32)
    outs = pl.pallas_call(
        functools.partial(kernel, ctx_size, dp_size),
        out_shape=tuple(pltpu.VMEM(shape, BF16) for shape in (block, block, block, part)),
        in_specs=[outer] * 10,
        out_specs=(inner,) * 4,
        scratch_shapes=[
            pltpu.VMEM(block, BF16),
            pltpu.VMEM(block, BF16),
            pltpu.VMEM(block, BF16),
            pltpu.VMEM(block, BF16),
            pltpu.VMEM((2 * ROWS, ROWS), BF16),
            pltpu.VMEM((ROWS, 2 * ROWS), BF16),
            pltpu.VMEM((2 * LANES, 2 * LANES), BF16),
            pltpu.VMEM((2 * LANES, 2 * LANES), BF16),
            pltpu.VMEM((ROWS, LANES), F32),
            pltpu.VMEM((ROWS, LANES), F32),
            pltpu.VMEM((6, ctx_size) + message, BF16),
            pltpu.VMEM((4, ctx_size) + message, BF16),
            pltpu.VMEM((lanes_x, share) + message, BF16),
            pltpu.VMEM((lanes_x, share) + message, BF16),
            pltpu.VMEM((share,) + message, BF16),
            pltpu.VMEM((2 * ctx_size // dp_size,) + message, BF16),
            pltpu.VMEM((ctx_size * OWN * UNITS, LANES), F32),
            pltpu.VMEM((2 * ROWS, OWN * LANES), F32),
            pltpu.VMEM((2 * ROWS, OWN * LANES), BF16),
            pltpu.VMEM((OWN * ROWS, 2 * LANES), BF16),
            spectrum,
            spectrum,
            spectrum,
            pltpu.SemaphoreType.DMA((8,)),
            pltpu.SemaphoreType.DMA((8,)),
            pltpu.SemaphoreType.DMA((10,)),
        ],
        compiler_params=pltpu.CompilerParams(
            collective_id=0, has_side_effects=True, vmem_limit_bytes=60 * 1024 * 1024
        ),
    )(
        signal.reshape(block),
        gate.reshape(block),
        filter_param,
        cotangent.reshape(block),
        *tables(),
    )
    outs = pl.pallas_call(
        hand_on,
        out_shape=tuple(jax.ShapeDtypeStruct(shape, BF16) for shape in (block, block, block, part)),
        in_specs=[inner] * 4,
        out_specs=(outer,) * 4,
        scratch_shapes=[pltpu.SemaphoreType.DMA((4,))],
        compiler_params=pltpu.CompilerParams(vmem_limit_bytes=4 * 1024 * 1024),
    )(*outs)
    return (outs[0][None], outs[1][None], outs[2][None], outs[3])


def solution(mesh):
    in_specs = (P("dp", None, "ctx"), P("dp", None, "ctx"), P(None, "ctx"), P("dp", None, "ctx"))
    out_specs = (P("dp", None, "ctx"), P("dp", None, "ctx"), P("dp", None, "ctx"), P("dp", "ctx"))
    return jax.shard_map(
        per_device, mesh=mesh, in_specs=in_specs, out_specs=out_specs, check_vma=False
    )
```

```python
import functools
import math

import jax
import jax.numpy as jnp
import numpy as np
from jax import lax
from jax.experimental import pallas as pl
from jax.experimental.pallas import tpu as pltpu
from jax.sharding import PartitionSpec as P

MESH = pl.DeviceIdType.MESH
F32 = jnp.float32
BF16 = jnp.bfloat16

LANES = 128
ROWS = 256
LENGTH = ROWS * LANES
OWN = 4
UNITS = 8
SCALE = float(LENGTH) ** -1.5


def tables():
    place = np.arange(ROWS, dtype=np.float64)
    lane = np.arange(LANES, dtype=np.float64)
    outer = 2.0 * math.pi / ROWS * (place[:, None] + 0.25) * place[None, :]
    first = np.concatenate([np.cos(outer), -np.sin(outer)], axis=0)
    turn = 2.0 * math.pi / LENGTH * (place[:, None] + 0.25) * lane[None, :]
    inner = 2.0 * math.pi / LANES * lane[:, None] * lane[None, :]
    cos, sin = np.cos(inner), np.sin(inner)
    second = np.concatenate(
        [np.concatenate([cos, -sin], axis=1), np.concatenate([sin, cos], axis=1)], axis=0
    )
    as_b = lambda member: jnp.asarray(member.astype(np.float32)).astype(BF16)
    return (
        as_b(first),
        as_b(first.T),
        as_b(second),
        as_b(second.T),
        jnp.asarray(np.cos(turn).astype(np.float32)),
        jnp.asarray(np.sin(turn).astype(np.float32)),
    )


def kernel(
    ctx_size,
    dp_size,
    signal_hbm,
    gate_hbm,
    filt_hbm,
    cot_hbm,
    first_hbm,
    first_t_hbm,
    second_hbm,
    second_t_hbm,
    turn_cos_hbm,
    turn_sin_hbm,
    gated,
    grad_signal,
    grad_gate,
    grad_filter,
    signal,
    gate,
    filt,
    cot,
    first,
    first_t,
    second,
    second_t,
    turn_cos,
    turn_sin,
    out_buf,
    in_buf,
    in_filt,
    out_part,
    in_part,
    out_sum,
    in_sum,
    stage,
    wide,
    lined,
    mixed,
    spec_h,
    spec_x,
    spec_g,
    send_sem,
    recv_sem,
    load_sem,
):
    me = lax.axis_index("ctx")
    row = lax.axis_index("dp")
    per_row = ctx_size // dp_size
    lanes_x = dp_size // 2
    my_x, my_z = row // 2, lax.rem(row, 2)
    share = ctx_size // lanes_x
    my_y, my_low = me // share, lax.rem(me, share) // 2
    SIG, MID, CNV, GRS, FIL, GRF = range(6)
    FIL_X, GRF_X = 6, 7

    loads = [
        pltpu.make_async_copy(source, target, load_sem.at[index])
        for index, (source, target) in enumerate(
            (
                (filt_hbm, filt),
                (signal_hbm, signal),
                (gate_hbm, gate),
                (cot_hbm, cot),
                (first_hbm, first),
                (turn_cos_hbm, turn_cos),
                (turn_sin_hbm, turn_sin),
                (second_hbm, second),
                (second_t_hbm, second_t),
                (first_t_hbm, first_t),
            )
        )
    ]

    def group_of(device):
        return lax.rem(device, 2) * (ctx_size // 2) + device // 2

    mine = group_of(me)

    barrier = pltpu.get_barrier_semaphore()

    def greet_ctx(step, carry):
        peer = lax.rem(me + step, ctx_size)
        pl.semaphore_signal(barrier, inc=1, device_id=(row, peer), device_id_type=MESH)
        return carry

    lax.fori_loop(1, ctx_size, greet_ctx, 0)
    for step in range(1, lanes_x):
        peer = lax.rem(my_x + step, lanes_x) * 2 + my_z
        pl.semaphore_signal(barrier, inc=1, device_id=(peer, me), device_id_type=MESH)
    other = my_x * 2 + 1 - my_z
    pl.semaphore_signal(barrier, inc=1, device_id=(other, me), device_id_type=MESH)

    for copy in loads:
        copy.start()

    def split_channels(which, block):
        for unit in range(UNITS):
            stage[pl.ds(unit, ctx_size * OWN, stride=UNITS), :] = block(
                pl.ds(unit * LANES, LANES)
            )
        out_buf[which] = stage[...].reshape(ctx_size, OWN * UNITS, LANES).astype(BF16)

    def remote(source, target, sem, device):
        pltpu.make_async_remote_copy(
            src_ref=source,
            dst_ref=target,
            send_sem=send_sem.at[sem],
            recv_sem=recv_sem.at[sem],
            device_id=device,
            device_id_type=MESH,
        ).start()

    def exchange(which):
        for apart in (2, 1, 3, 0):
            low = lax.rem(my_low + apart, share // 2)

            def send(step, carry, low=low):
                far_y = lax.rem(my_y + 2 + step // 2, lanes_x)
                peer = far_y * share + low * 2 + lax.rem(me + step, 2)
                leaving, landing = (group_of(peer), me) if which in (SIG, MID) else (peer, mine)
                remote(
                    out_buf.at[which, leaving], in_buf.at[which, landing], which, (row, peer)
                )
                return carry

            if apart:
                lax.fori_loop(0, share, send, 0)
            else:
                lax.fori_loop(0, share // 2, send, 0)
                lax.fori_loop(share // 2 + 1, share, send, 0)
        if which in (SIG, MID):
            in_buf[which, me] = out_buf[which, mine]
        else:
            in_buf[which, mine] = out_buf[which, me]

    def wait_for(sem, which, count):
        part = in_buf.at[0, pl.ds(0, count)]
        pltpu.make_async_copy(part, part, sem.at[which]).wait()

    def wait_either(sem, which, count, less):
        @pl.when(less)
        def _():
            wait_for(sem, which, count - 1)

        @pl.when(jnp.logical_not(less))
        def _():
            wait_for(sem, which, count)

    def line_up(part, block, blocks):
        part = part.astype(F32)
        for own in range(OWN):
            rows = part[:, own * UNITS : (own + 1) * UNITS, :].reshape(blocks * UNITS, LANES)
            lined[
                block * UNITS : (block + blocks) * UNITS, own * LANES : (own + 1) * LANES
            ] = rows.astype(BF16)

    def transform(spec):
        wide[...] = jnp.dot(first[...], lined[0:ROWS, :], preferred_element_type=F32)
        for own in range(OWN):
            lanes = slice(own * LANES, (own + 1) * LANES)
            rows = slice(own * ROWS, (own + 1) * ROWS)
            real, imag = wide[0:ROWS, lanes], wide[ROWS : 2 * ROWS, lanes]
            cos, sin = turn_cos[...], turn_sin[...]
            mixed[rows, 0:LANES] = (real * cos + imag * sin).astype(BF16)
            mixed[rows, LANES : 2 * LANES] = (imag * cos - real * sin).astype(BF16)
        spec[...] = jnp.dot(mixed[...], second[...], preferred_element_type=F32)

    def multiply(left, right, conjugate):
        for own in range(OWN):
            rows = slice(own * ROWS, (own + 1) * ROWS)
            left_re, left_im = left[rows, 0:LANES], left[rows, LANES : 2 * LANES]
            right_re, right_im = right[rows, 0:LANES], right[rows, LANES : 2 * LANES]
            if conjugate:
                real = left_re * right_re + left_im * right_im
                imag = left_re * right_im - left_im * right_re
            else:
                real = left_re * right_re - left_im * right_im
                imag = left_re * right_im + left_im * right_re
            mixed[rows, 0:LANES] = real.astype(BF16)
            mixed[rows, LANES : 2 * LANES] = imag.astype(BF16)

    def transform_back(which):
        for own in range(OWN):
            lanes = slice(own * LANES, (own + 1) * LANES)
            rows = slice(own * ROWS, (own + 1) * ROWS)
            both = jnp.dot(mixed[rows, :], second_t[...], preferred_element_type=F32)
            real, imag = both[:, 0:LANES], both[:, LANES : 2 * LANES]
            cos, sin = turn_cos[...], turn_sin[...]
            lined[0:ROWS, lanes] = (real * cos - imag * sin).astype(BF16)
            lined[ROWS : 2 * ROWS, lanes] = (real * sin + imag * cos).astype(BF16)
        values = jnp.dot(first_t[...], lined[...], preferred_element_type=F32) * SCALE
        parts = [
            values[:, own * LANES : (own + 1) * LANES].reshape(ctx_size, UNITS, LANES)
            for own in range(OWN)
        ]
        message = jnp.concatenate(parts, axis=1).astype(BF16)
        if which != GRF:
            out_buf[which] = message
            return
        for pair in range(ctx_size // 2):
            part_y, part_low = pair // (share // 2), pair % (share // 2)
            group = (part_y + part_low) % lanes_x
            out_part[group, 2 * part_y : 2 * part_y + 2] = message[2 * pair : 2 * pair + 2]

    diagonal = my_y + my_low
    filt_slot = 2 * my_y + lax.rem(me, 2)
    fetches_own = lax.rem(2 * diagonal, lanes_x) == my_x

    loads[0].wait()
    split_channels(FIL, lambda lanes: filt[:, lanes].astype(F32))
    loads[1].wait()
    split_channels(SIG, lambda lanes: signal[:, lanes].astype(F32))
    pl.semaphore_wait(barrier, ctx_size - 1 + lanes_x)

    def send_filter(step, carry):
        far_y = lax.rem(my_y + 2 + step // 2, lanes_x)
        low = lax.rem(my_x + 3 * lanes_x - diagonal - far_y, lanes_x)
        peer = far_y * share + low * 2 + lax.rem(me + step, 2)

        @pl.when(peer != me)
        def _():
            leaving = out_buf.at[FIL, group_of(peer)]
            remote(leaving, in_filt.at[my_x, filt_slot], FIL, (row, peer))

        return carry

    lax.fori_loop(0, share, send_filter, 0)

    @pl.when(fetches_own)
    def _():
        in_filt[my_x, filt_slot] = out_buf[FIL, mine]

    exchange(SIG)
    loads[2].wait()
    loads[3].wait()
    split_channels(MID, lambda lanes: gate[:, lanes].astype(F32) * cot[:, lanes].astype(F32))
    wait_either(recv_sem, FIL, share, fetches_own)
    for step in range(1, lanes_x):
        peer = lax.rem(my_x + step, lanes_x) * 2 + my_z
        remote(in_filt.at[my_x], in_filt.at[my_x], FIL_X, (peer, me))
    exchange(MID)

    for copy in loads[4:]:
        copy.wait()
    wait_for(recv_sem, SIG, ctx_size - 1)
    line_up(in_buf[SIG], 0, ctx_size)
    transform(spec_x)
    wait_for(recv_sem, FIL_X, share * (lanes_x - 1))
    for pair in range(ctx_size // 2):
        part_y, part_low = pair // (share // 2), pair % (share // 2)
        group = lax.rem(part_y + part_low + diagonal, lanes_x)
        line_up(in_filt[group, 2 * part_y : 2 * part_y + 2], 2 * pair, 2)
    transform(spec_h)
    multiply(spec_h, spec_x, False)
    transform_back(CNV)
    exchange(CNV)

    wait_for(recv_sem, MID, ctx_size - 1)
    line_up(in_buf[MID], 0, ctx_size)
    transform(spec_g)
    multiply(spec_x, spec_g, True)
    transform_back(GRF)
    for step in range(1, lanes_x):
        peer = lax.rem(my_x + step, lanes_x)
        remote(out_part.at[peer], in_part.at[my_x], GRF_X, (peer * 2 + my_z, me))
    in_part[my_x] = out_part[my_x]

    multiply(spec_h, spec_g, True)
    transform_back(GRS)
    exchange(GRS)

    wait_for(recv_sem, GRF_X, share * (lanes_x - 1))
    total = in_part[0].astype(F32)
    for part in range(1, lanes_x):
        total = total + in_part[part].astype(F32)
    out_sum[...] = total.astype(BF16)
    to_row = mine // per_row
    slot = my_z * per_row + lax.rem(mine, per_row)
    stays = jnp.logical_and(to_row == row, lax.rem(diagonal, lanes_x) == my_x)

    def send_sum(block, carry):
        far_y = block // 2
        low = lax.rem(my_x + lanes_x - far_y, lanes_x)
        peer = far_y * share + low * 2 + lax.rem(block, 2)
        leaves = jnp.logical_or(to_row != row, peer != me)

        @pl.when(leaves)
        def _():
            remote(out_sum.at[block], in_sum.at[slot], GRF, (to_row, peer))

        return carry

    lax.fori_loop(0, share, send_sum, 0)

    @pl.when(stays)
    def _():
        in_sum[slot] = out_sum[filt_slot]

    wait_for(recv_sem, CNV, ctx_size - 1)
    stage[...] = in_buf[CNV].astype(F32).reshape(ctx_size * OWN * UNITS, LANES)
    for unit in range(UNITS):
        lanes = pl.ds(unit * LANES, LANES)
        conv = stage[pl.ds(unit, ctx_size * OWN, stride=UNITS), :]
        gated[:, lanes] = (gate[:, lanes].astype(F32) * conv).astype(BF16)
        grad_gate[:, lanes] = (cot[:, lanes].astype(F32) * conv).astype(BF16)

    wait_either(recv_sem, GRF, 2 * per_row, stays)
    total = in_sum[0:per_row].astype(F32) + in_sum[per_row : 2 * per_row].astype(F32)
    stage[0 : per_row * OWN * UNITS, :] = total.reshape(per_row * OWN * UNITS, LANES)
    for unit in range(UNITS):
        lanes = pl.ds(unit * LANES, LANES)
        grad_filter[:, lanes] = stage[pl.ds(unit, per_row * OWN, stride=UNITS), :].astype(BF16)

    wait_for(recv_sem, GRS, ctx_size - 1)
    stage[...] = in_buf[GRS].astype(F32).reshape(ctx_size * OWN * UNITS, LANES)
    for unit in range(UNITS):
        lanes = pl.ds(unit * LANES, LANES)
        grad_signal[:, lanes] = stage[pl.ds(unit, ctx_size * OWN, stride=UNITS), :].astype(BF16)

    for which in (SIG, MID, CNV, GRS):
        wait_for(send_sem, which, ctx_size - 1)
    for which in (FIL_X, GRF_X):
        wait_for(send_sem, which, share * (lanes_x - 1))
    wait_either(send_sem, GRF, share, stays)
    wait_either(send_sem, FIL, share, fetches_own)


def hand_on(*refs):
    sources, targets, sem = refs[0:4], refs[4:8], refs[8]
    copies = [
        pltpu.make_async_copy(source, target, sem.at[index])
        for index, (source, target) in enumerate(zip(sources, targets))
    ]
    for copy in copies:
        copy.start()
    for copy in copies:
        copy.wait()


def per_device(signal, gate, filter_param, cotangent):
    ctx_size = lax.axis_size("ctx")
    dp_size = lax.axis_size("dp")
    channels, length = filter_param.shape
    lanes_x = dp_size // 2
    share = ctx_size // lanes_x
    block = (channels, length)
    part = (channels // dp_size, length)
    outer = pl.BlockSpec(memory_space=pltpu.HBM)
    inner = pl.BlockSpec(memory_space=pltpu.VMEM)
    message = (OWN * UNITS, LANES)
    spectrum = pltpu.VMEM((OWN * ROWS, 2 * LANES), F32)
    outs = pl.pallas_call(
        functools.partial(kernel, ctx_size, dp_size),
        out_shape=tuple(pltpu.VMEM(shape, BF16) for shape in (block, block, block, part)),
        in_specs=[outer] * 10,
        out_specs=(inner,) * 4,
        scratch_shapes=[
            pltpu.VMEM(block, BF16),
            pltpu.VMEM(block, BF16),
            pltpu.VMEM(block, BF16),
            pltpu.VMEM(block, BF16),
            pltpu.VMEM((2 * ROWS, ROWS), BF16),
            pltpu.VMEM((ROWS, 2 * ROWS), BF16),
            pltpu.VMEM((2 * LANES, 2 * LANES), BF16),
            pltpu.VMEM((2 * LANES, 2 * LANES), BF16),
            pltpu.VMEM((ROWS, LANES), F32),
            pltpu.VMEM((ROWS, LANES), F32),
            pltpu.VMEM((5, ctx_size) + message, BF16),
            pltpu.VMEM((4, ctx_size) + message, BF16),
            pltpu.VMEM((lanes_x, share) + message, BF16),
            pltpu.VMEM((lanes_x, share) + message, BF16),
            pltpu.VMEM((lanes_x, share) + message, BF16),
            pltpu.VMEM((share,) + message, BF16),
            pltpu.VMEM((2 * ctx_size // dp_size,) + message, BF16),
            pltpu.VMEM((ctx_size * OWN * UNITS, LANES), F32),
            pltpu.VMEM((2 * ROWS, OWN * LANES), F32),
            pltpu.VMEM((2 * ROWS, OWN * LANES), BF16),
            pltpu.VMEM((OWN * ROWS, 2 * LANES), BF16),
            spectrum,
            spectrum,
            spectrum,
            pltpu.SemaphoreType.DMA((8,)),
            pltpu.SemaphoreType.DMA((8,)),
            pltpu.SemaphoreType.DMA((10,)),
        ],
        compiler_params=pltpu.CompilerParams(
            collective_id=0, has_side_effects=True, vmem_limit_bytes=60 * 1024 * 1024
        ),
    )(
        signal.reshape(block),
        gate.reshape(block),
        filter_param,
        cotangent.reshape(block),
        *tables(),
    )
    outs = pl.pallas_call(
        hand_on,
        out_shape=tuple(jax.ShapeDtypeStruct(shape, BF16) for shape in (block, block, block, part)),
        in_specs=[inner] * 4,
        out_specs=(outer,) * 4,
        scratch_shapes=[pltpu.SemaphoreType.DMA((4,))],
        compiler_params=pltpu.CompilerParams(vmem_limit_bytes=4 * 1024 * 1024),
    )(*outs)
    return (outs[0][None], outs[1][None], outs[2][None], outs[3])


def solution(mesh):
    in_specs = (P("dp", None, "ctx"), P("dp", None, "ctx"), P(None, "ctx"), P("dp", None, "ctx"))
    out_specs = (P("dp", None, "ctx"), P("dp", None, "ctx"), P("dp", None, "ctx"), P("dp", "ctx"))
    return jax.shard_map(
        per_device, mesh=mesh, in_specs=in_specs, out_specs=out_specs, check_vma=False
    )
```

```python
import functools
import math

import jax
import jax.numpy as jnp
import numpy as np
from jax import lax
from jax.experimental import pallas as pl
from jax.experimental.pallas import tpu as pltpu
from jax.sharding import PartitionSpec as P

MESH = pl.DeviceIdType.MESH
F32 = jnp.float32
BF16 = jnp.bfloat16

LANES = 128
ROWS = 256
LENGTH = ROWS * LANES
OWN = 4
UNITS = 8
SCALE = float(LENGTH) ** -1.5


def tables():
    place = np.arange(ROWS, dtype=np.float64)
    lane = np.arange(LANES, dtype=np.float64)
    outer = 2.0 * math.pi / ROWS * (place[:, None] + 0.25) * place[None, :]
    first = np.concatenate([np.cos(outer), -np.sin(outer)], axis=0)
    turn = 2.0 * math.pi / LENGTH * (place[:, None] + 0.25) * lane[None, :]
    inner = 2.0 * math.pi / LANES * lane[:, None] * lane[None, :]
    cos, sin = np.cos(inner), np.sin(inner)
    second = np.concatenate(
        [np.concatenate([cos, -sin], axis=1), np.concatenate([sin, cos], axis=1)], axis=0
    )
    as_b = lambda member: jnp.asarray(member.astype(np.float32)).astype(BF16)
    return (
        as_b(first),
        as_b(first.T),
        as_b(second),
        as_b(second.T),
        jnp.asarray(np.cos(turn).astype(np.float32)),
        jnp.asarray(np.sin(turn).astype(np.float32)),
    )


def kernel(
    ctx_size,
    dp_size,
    signal_hbm,
    gate_hbm,
    filt_hbm,
    cot_hbm,
    first_hbm,
    first_t_hbm,
    second_hbm,
    second_t_hbm,
    turn_cos_hbm,
    turn_sin_hbm,
    gated,
    grad_signal,
    grad_gate,
    grad_filter,
    signal,
    gate,
    filt,
    cot,
    first,
    first_t,
    second,
    second_t,
    turn_cos,
    turn_sin,
    out_buf,
    in_buf,
    in_filt,
    out_part,
    in_part,
    out_sum,
    in_sum,
    stage,
    wide,
    lined,
    mixed,
    spec_h,
    spec_x,
    spec_g,
    send_sem,
    recv_sem,
    load_sem,
):
    me = lax.axis_index("ctx")
    row = lax.axis_index("dp")
    per_row = ctx_size // dp_size
    lanes_x = dp_size // 2
    my_x, my_z = row // 2, lax.rem(row, 2)
    share = ctx_size // lanes_x
    my_y, my_low = me // share, lax.rem(me, share) // 2
    SIG, MID, CNV, GRS, FIL, GRF = range(6)
    FIL_X, GRF_X = 6, 7

    loads = [
        pltpu.make_async_copy(source, target, load_sem.at[index])
        for index, (source, target) in enumerate(
            (
                (filt_hbm, filt),
                (signal_hbm, signal),
                (gate_hbm, gate),
                (cot_hbm, cot),
                (first_hbm, first),
                (turn_cos_hbm, turn_cos),
                (turn_sin_hbm, turn_sin),
                (second_hbm, second),
                (second_t_hbm, second_t),
                (first_t_hbm, first_t),
            )
        )
    ]

    for copy in loads[0:2]:
        copy.start()

    def group_of(device):
        return 16 * (lax.rem(device, 2)) + 8 * (lax.rem(device // 4, 2)) + 4 * (lax.rem(device // 2, 2)) + 2 * (device // 16) + 1 * (lax.rem(device // 8, 2))

    mine = group_of(me)

    barrier = pltpu.get_barrier_semaphore()

    def greet_ctx(step, carry):
        peer = lax.rem(me + step, ctx_size)
        pl.semaphore_signal(barrier, inc=1, device_id=(row, peer), device_id_type=MESH)
        return carry

    lax.fori_loop(1, ctx_size, greet_ctx, 0)
    for step in range(1, lanes_x):
        peer = lax.rem(my_x + step, lanes_x) * 2 + my_z
        pl.semaphore_signal(barrier, inc=1, device_id=(peer, me), device_id_type=MESH)
    other = my_x * 2 + 1 - my_z
    pl.semaphore_signal(barrier, inc=1, device_id=(other, me), device_id_type=MESH)

    for copy in loads[2:]:
        copy.start()

    def split_channels(which, block):
        for unit in range(UNITS):
            stage[pl.ds(unit, ctx_size * OWN, stride=UNITS), :] = block(
                pl.ds(unit * LANES, LANES)
            )
        out_buf[which] = stage[...].reshape(ctx_size, OWN * UNITS, LANES).astype(BF16)

    def remote(source, target, sem, device):
        pltpu.make_async_remote_copy(
            src_ref=source,
            dst_ref=target,
            send_sem=send_sem.at[sem],
            recv_sem=recv_sem.at[sem],
            device_id=device,
            device_id_type=MESH,
        ).start()

    def exchange(which):
        for apart in (2, 1, 3, 0):
            low = lax.rem(my_low + apart, share // 2)

            def send(step, carry, low=low):
                far_y = lax.rem(my_y + 2 + step // 2, lanes_x)
                peer = far_y * share + low * 2 + lax.rem(me + step, 2)
                leaving, landing = (group_of(peer), me) if which in (SIG, MID) else (peer, mine)
                remote(
                    out_buf.at[which, leaving], in_buf.at[which, landing], which, (row, peer)
                )
                return carry

            if apart:
                lax.fori_loop(0, share, send, 0)
            else:
                lax.fori_loop(0, share // 2, send, 0)
                lax.fori_loop(share // 2 + 1, share, send, 0)
        if which in (SIG, MID):
            in_buf[which, me] = out_buf[which, mine]
        else:
            in_buf[which, mine] = out_buf[which, me]

    def wait_for(sem, which, count):
        part = in_buf.at[0, pl.ds(0, count)]
        pltpu.make_async_copy(part, part, sem.at[which]).wait()

    def wait_either(sem, which, count, less):
        @pl.when(less)
        def _():
            wait_for(sem, which, count - 1)

        @pl.when(jnp.logical_not(less))
        def _():
            wait_for(sem, which, count)

    def line_up(part, block, blocks):
        part = part.astype(F32)
        for own in range(OWN):
            rows = part[:, own * UNITS : (own + 1) * UNITS, :].reshape(blocks * UNITS, LANES)
            lined[
                block * UNITS : (block + blocks) * UNITS, own * LANES : (own + 1) * LANES
            ] = rows.astype(BF16)

    def transform(spec):
        wide[...] = jnp.dot(first[...], lined[0:ROWS, :], preferred_element_type=F32)
        for own in range(OWN):
            lanes = slice(own * LANES, (own + 1) * LANES)
            rows = slice(own * ROWS, (own + 1) * ROWS)
            real, imag = wide[0:ROWS, lanes], wide[ROWS : 2 * ROWS, lanes]
            cos, sin = turn_cos[...], turn_sin[...]
            mixed[rows, 0:LANES] = (real * cos + imag * sin).astype(BF16)
            mixed[rows, LANES : 2 * LANES] = (imag * cos - real * sin).astype(BF16)
        spec[...] = jnp.dot(mixed[...], second[...], preferred_element_type=F32)

    def multiply(left, right, conjugate):
        for own in range(OWN):
            rows = slice(own * ROWS, (own + 1) * ROWS)
            left_re, left_im = left[rows, 0:LANES], left[rows, LANES : 2 * LANES]
            right_re, right_im = right[rows, 0:LANES], right[rows, LANES : 2 * LANES]
            if conjugate:
                real = left_re * right_re + left_im * right_im
                imag = left_re * right_im - left_im * right_re
            else:
                real = left_re * right_re - left_im * right_im
                imag = left_re * right_im + left_im * right_re
            mixed[rows, 0:LANES] = real.astype(BF16)
            mixed[rows, LANES : 2 * LANES] = imag.astype(BF16)

    def transform_back(which):
        for own in range(OWN):
            lanes = slice(own * LANES, (own + 1) * LANES)
            rows = slice(own * ROWS, (own + 1) * ROWS)
            both = jnp.dot(mixed[rows, :], second_t[...], preferred_element_type=F32)
            real, imag = both[:, 0:LANES], both[:, LANES : 2 * LANES]
            cos, sin = turn_cos[...], turn_sin[...]
            lined[0:ROWS, lanes] = (real * cos - imag * sin).astype(BF16)
            lined[ROWS : 2 * ROWS, lanes] = (real * sin + imag * cos).astype(BF16)
        values = jnp.dot(first_t[...], lined[...], preferred_element_type=F32) * SCALE
        parts = [
            values[:, own * LANES : (own + 1) * LANES].reshape(ctx_size, UNITS, LANES)
            for own in range(OWN)
        ]
        message = jnp.concatenate(parts, axis=1).astype(BF16)
        if which != GRF:
            out_buf[which] = message
            return
        for pair in range(ctx_size // 2):
            part_y, part_low = pair // (share // 2), pair % (share // 2)
            group = (part_y + part_low) % lanes_x
            out_part[group, 2 * part_y : 2 * part_y + 2] = message[2 * pair : 2 * pair + 2]

    diagonal = my_y + my_low
    filt_slot = 2 * my_y + lax.rem(me, 2)
    fetches_own = lax.rem(2 * diagonal, lanes_x) == my_x

    loads[0].wait()
    split_channels(FIL, lambda lanes: filt[:, lanes].astype(F32))
    pl.semaphore_wait(barrier, ctx_size - 1 + lanes_x)

    def send_filter(step, carry):
        far_y = lax.rem(my_y + 2 + step // 2, lanes_x)
        low = lax.rem(my_x + 3 * lanes_x - diagonal - far_y, lanes_x)
        peer = far_y * share + low * 2 + lax.rem(me + step, 2)

        @pl.when(peer != me)
        def _():
            leaving = out_buf.at[FIL, group_of(peer)]
            remote(leaving, in_filt.at[my_x, filt_slot], FIL, (row, peer))

        return carry

    lax.fori_loop(0, share, send_filter, 0)

    @pl.when(fetches_own)
    def _():
        in_filt[my_x, filt_slot] = out_buf[FIL, mine]

    loads[1].wait()
    split_channels(SIG, lambda lanes: signal[:, lanes].astype(F32))
    exchange(SIG)
    loads[2].wait()
    loads[3].wait()
    split_channels(MID, lambda lanes: gate[:, lanes].astype(F32) * cot[:, lanes].astype(F32))
    wait_either(recv_sem, FIL, share, fetches_own)
    for step in range(1, lanes_x):
        peer = lax.rem(my_x + step, lanes_x) * 2 + my_z
        remote(in_filt.at[my_x], in_filt.at[my_x], FIL_X, (peer, me))
    exchange(MID)

    for copy in loads[4:]:
        copy.wait()
    wait_for(recv_sem, SIG, ctx_size - 1)
    line_up(in_buf[SIG], 0, ctx_size)
    transform(spec_x)
    wait_for(recv_sem, FIL_X, share * (lanes_x - 1))
    for pair in range(ctx_size // 2):
        part_y, part_low = pair // (share // 2), pair % (share // 2)
        group = lax.rem(part_y + part_low + diagonal, lanes_x)
        line_up(in_filt[group, 2 * part_y : 2 * part_y + 2], 2 * pair, 2)
    transform(spec_h)
    multiply(spec_h, spec_x, False)
    transform_back(CNV)
    exchange(CNV)

    wait_for(recv_sem, MID, ctx_size - 1)
    line_up(in_buf[MID], 0, ctx_size)
    transform(spec_g)
    multiply(spec_x, spec_g, True)
    transform_back(GRF)
    for part_y in range(lanes_x):
        for step in range(1, lanes_x):
            peer = lax.rem(my_x + step, lanes_x)
            blocks = pl.ds(2 * part_y, 2)
            remote(
                out_part.at[peer, blocks],
                in_part.at[my_x, blocks],
                GRF_X + part_y,
                (peer * 2 + my_z, me),
            )
    in_part[my_x] = out_part[my_x]

    multiply(spec_h, spec_g, True)
    transform_back(GRS)
    exchange(GRS)

    to_row = mine // per_row
    slot = my_z * per_row + lax.rem(mine, per_row)
    stays = jnp.logical_and(to_row == row, lax.rem(diagonal, lanes_x) == my_x)

    def send_sums(part_y):
        wait_for(recv_sem, GRF_X + part_y, 2 * (lanes_x - 1))
        blocks = slice(2 * part_y, 2 * part_y + 2)
        total = in_part[0, blocks].astype(F32)
        for part in range(1, lanes_x):
            total = total + in_part[part, blocks].astype(F32)
        out_sum[blocks] = total.astype(BF16)
        low = lax.rem(my_x + lanes_x - part_y, lanes_x)
        for block in (2 * part_y, 2 * part_y + 1):
            peer = part_y * share + low * 2 + block % 2
            leaves = jnp.logical_or(to_row != row, peer != me)

            @pl.when(leaves)
            def _(block=block, peer=peer):
                remote(out_sum.at[block], in_sum.at[slot], GRF, (to_row, peer))

    for part_y in range(lanes_x):
        send_sums(part_y)

    @pl.when(stays)
    def _():
        in_sum[slot] = out_sum[filt_slot]

    wait_for(recv_sem, CNV, ctx_size - 1)
    stage[...] = in_buf[CNV].astype(F32).reshape(ctx_size * OWN * UNITS, LANES)
    for unit in range(UNITS):
        lanes = pl.ds(unit * LANES, LANES)
        conv = stage[pl.ds(unit, ctx_size * OWN, stride=UNITS), :]
        gated[:, lanes] = (gate[:, lanes].astype(F32) * conv).astype(BF16)
        grad_gate[:, lanes] = (cot[:, lanes].astype(F32) * conv).astype(BF16)

    wait_either(recv_sem, GRF, 2 * per_row, stays)
    total = in_sum[0:per_row].astype(F32) + in_sum[per_row : 2 * per_row].astype(F32)
    stage[0 : per_row * OWN * UNITS, :] = total.reshape(per_row * OWN * UNITS, LANES)
    for unit in range(UNITS):
        lanes = pl.ds(unit * LANES, LANES)
        grad_filter[:, lanes] = stage[pl.ds(unit, per_row * OWN, stride=UNITS), :].astype(BF16)

    wait_for(recv_sem, GRS, ctx_size - 1)
    stage[...] = in_buf[GRS].astype(F32).reshape(ctx_size * OWN * UNITS, LANES)
    for unit in range(UNITS):
        lanes = pl.ds(unit * LANES, LANES)
        grad_signal[:, lanes] = stage[pl.ds(unit, ctx_size * OWN, stride=UNITS), :].astype(BF16)

    for which in (SIG, MID, CNV, GRS):
        wait_for(send_sem, which, ctx_size - 1)
    wait_for(send_sem, FIL_X, share * (lanes_x - 1))
    for part_y in range(lanes_x):
        wait_for(send_sem, GRF_X + part_y, 2 * (lanes_x - 1))
    wait_either(send_sem, GRF, share, stays)
    wait_either(send_sem, FIL, share, fetches_own)


def hand_on(*refs):
    sources, targets, sem = refs[0:4], refs[4:8], refs[8]
    copies = [
        pltpu.make_async_copy(source, target, sem.at[index])
        for index, (source, target) in enumerate(zip(sources, targets))
    ]
    for copy in copies:
        copy.start()
    for copy in copies:
        copy.wait()


def per_device(signal, gate, filter_param, cotangent):
    ctx_size = lax.axis_size("ctx")
    dp_size = lax.axis_size("dp")
    channels, length = filter_param.shape
    lanes_x = dp_size // 2
    share = ctx_size // lanes_x
    block = (channels, length)
    part = (channels // dp_size, length)
    outer = pl.BlockSpec(memory_space=pltpu.HBM)
    inner = pl.BlockSpec(memory_space=pltpu.VMEM)
    message = (OWN * UNITS, LANES)
    spectrum = pltpu.VMEM((OWN * ROWS, 2 * LANES), F32)
    outs = pl.pallas_call(
        functools.partial(kernel, ctx_size, dp_size),
        out_shape=tuple(pltpu.VMEM(shape, BF16) for shape in (block, block, block, part)),
        in_specs=[outer] * 10,
        out_specs=(inner,) * 4,
        scratch_shapes=[
            pltpu.VMEM(block, BF16),
            pltpu.VMEM(block, BF16),
            pltpu.VMEM(block, BF16),
            pltpu.VMEM(block, BF16),
            pltpu.VMEM((2 * ROWS, ROWS), BF16),
            pltpu.VMEM((ROWS, 2 * ROWS), BF16),
            pltpu.VMEM((2 * LANES, 2 * LANES), BF16),
            pltpu.VMEM((2 * LANES, 2 * LANES), BF16),
            pltpu.VMEM((ROWS, LANES), F32),
            pltpu.VMEM((ROWS, LANES), F32),
            pltpu.VMEM((5, ctx_size) + message, BF16),
            pltpu.VMEM((4, ctx_size) + message, BF16),
            pltpu.VMEM((lanes_x, share) + message, BF16),
            pltpu.VMEM((lanes_x, share) + message, BF16),
            pltpu.VMEM((lanes_x, share) + message, BF16),
            pltpu.VMEM((share,) + message, BF16),
            pltpu.VMEM((2 * ctx_size // dp_size,) + message, BF16),
            pltpu.VMEM((ctx_size * OWN * UNITS, LANES), F32),
            pltpu.VMEM((2 * ROWS, OWN * LANES), F32),
            pltpu.VMEM((2 * ROWS, OWN * LANES), BF16),
            pltpu.VMEM((OWN * ROWS, 2 * LANES), BF16),
            spectrum,
            spectrum,
            spectrum,
            pltpu.SemaphoreType.DMA((7 + lanes_x,)),
            pltpu.SemaphoreType.DMA((7 + lanes_x,)),
            pltpu.SemaphoreType.DMA((10,)),
        ],
        compiler_params=pltpu.CompilerParams(
            collective_id=0, has_side_effects=True, vmem_limit_bytes=60 * 1024 * 1024
        ),
    )(
        signal.reshape(block),
        gate.reshape(block),
        filter_param,
        cotangent.reshape(block),
        *tables(),
    )
    outs = pl.pallas_call(
        hand_on,
        out_shape=tuple(jax.ShapeDtypeStruct(shape, BF16) for shape in (block, block, block, part)),
        in_specs=[inner] * 4,
        out_specs=(outer,) * 4,
        scratch_shapes=[pltpu.SemaphoreType.DMA((4,))],
        compiler_params=pltpu.CompilerParams(vmem_limit_bytes=4 * 1024 * 1024),
    )(*outs)
    return (outs[0][None], outs[1][None], outs[2][None], outs[3])


def solution(mesh):
    in_specs = (P("dp", None, "ctx"), P("dp", None, "ctx"), P(None, "ctx"), P("dp", None, "ctx"))
    out_specs = (P("dp", None, "ctx"), P("dp", None, "ctx"), P("dp", None, "ctx"), P("dp", "ctx"))
    return jax.shard_map(
        per_device, mesh=mesh, in_specs=in_specs, out_specs=out_specs, check_vma=False
    )
```

```python
import functools
import math

import jax
import jax.numpy as jnp
import numpy as np
from jax import lax
from jax.experimental import pallas as pl
from jax.experimental.pallas import tpu as pltpu
from jax.sharding import PartitionSpec as P

MESH = pl.DeviceIdType.MESH
F32 = jnp.float32
BF16 = jnp.bfloat16

LANES = 128
ROWS = 256
LENGTH = ROWS * LANES
OWN = 4
UNITS = 8
SCALE = float(LENGTH) ** -1.5


def tables():
    place = np.arange(ROWS, dtype=np.float64)
    lane = np.arange(LANES, dtype=np.float64)
    outer = 2.0 * math.pi / ROWS * (place[:, None] + 0.25) * place[None, :]
    first = np.concatenate([np.cos(outer), -np.sin(outer)], axis=0)
    turn = 2.0 * math.pi / LENGTH * (place[:, None] + 0.25) * lane[None, :]
    inner = 2.0 * math.pi / LANES * lane[:, None] * lane[None, :]
    cos, sin = np.cos(inner), np.sin(inner)
    second = np.concatenate(
        [np.concatenate([cos, -sin], axis=1), np.concatenate([sin, cos], axis=1)], axis=0
    )
    as_b = lambda member: jnp.asarray(member.astype(np.float32)).astype(BF16)
    return (
        as_b(first),
        as_b(first.T),
        as_b(second),
        as_b(second.T),
        jnp.asarray(np.cos(turn).astype(np.float32)),
        jnp.asarray(np.sin(turn).astype(np.float32)),
    )


def kernel(
    ctx_size,
    dp_size,
    signal_hbm,
    gate_hbm,
    filt_hbm,
    cot_hbm,
    first_hbm,
    first_t_hbm,
    second_hbm,
    second_t_hbm,
    turn_cos_hbm,
    turn_sin_hbm,
    gated,
    grad_signal,
    grad_gate,
    grad_filter,
    signal,
    gate,
    filt,
    cot,
    first,
    first_t,
    second,
    second_t,
    turn_cos,
    turn_sin,
    out_buf,
    in_buf,
    in_filt,
    out_part,
    in_part,
    out_sum,
    in_sum,
    stage,
    wide,
    lined,
    mixed,
    spec_h,
    spec_x,
    spec_g,
    send_sem,
    recv_sem,
    load_sem,
):
    me = lax.axis_index("ctx")
    row = lax.axis_index("dp")
    per_row = ctx_size // dp_size
    lanes_x = dp_size // 2
    my_x, my_z = row // 2, lax.rem(row, 2)
    share = ctx_size // lanes_x
    my_y, my_low = me // share, lax.rem(me, share) // 2
    SIG, MID, CNV, GRS, FIL, GRF = range(6)
    FIL_X, GRF_X = 6, 7

    loads = [
        pltpu.make_async_copy(source, target, load_sem.at[index])
        for index, (source, target) in enumerate(
            (
                (filt_hbm, filt),
                (signal_hbm, signal),
                (gate_hbm, gate),
                (cot_hbm, cot),
                (first_hbm, first),
                (turn_cos_hbm, turn_cos),
                (turn_sin_hbm, turn_sin),
                (second_hbm, second),
                (second_t_hbm, second_t),
                (first_t_hbm, first_t),
            )
        )
    ]

    for copy in loads[0:2]:
        copy.start()

    def group_of(device):
        return 16 * (lax.rem(device, 2)) + 8 * (lax.rem(device // 8, 2)) + 4 * (lax.rem(device // 2, 2)) + 2 * (device // 16) + 1 * (lax.rem(device // 4, 2))

    mine = group_of(me)

    barrier = pltpu.get_barrier_semaphore()

    def greet_ctx(step, carry):
        peer = lax.rem(me + step, ctx_size)
        pl.semaphore_signal(barrier, inc=1, device_id=(row, peer), device_id_type=MESH)
        return carry

    lax.fori_loop(1, ctx_size, greet_ctx, 0)
    for step in range(1, lanes_x):
        peer = lax.rem(my_x + step, lanes_x) * 2 + my_z
        pl.semaphore_signal(barrier, inc=1, device_id=(peer, me), device_id_type=MESH)
    other = my_x * 2 + 1 - my_z
    pl.semaphore_signal(barrier, inc=1, device_id=(other, me), device_id_type=MESH)

    for copy in loads[2:]:
        copy.start()

    def split_channels(which, block):
        for unit in range(UNITS):
            stage[pl.ds(unit, ctx_size * OWN, stride=UNITS), :] = block(
                pl.ds(unit * LANES, LANES)
            )
        out_buf[which] = stage[...].reshape(ctx_size, OWN * UNITS, LANES).astype(BF16)

    def remote(source, target, sem, device):
        pltpu.make_async_remote_copy(
            src_ref=source,
            dst_ref=target,
            send_sem=send_sem.at[sem],
            recv_sem=recv_sem.at[sem],
            device_id=device,
            device_id_type=MESH,
        ).start()

    def exchange(which):
        for apart in (2, 1, 3, 0):
            low = lax.rem(my_low + apart, share // 2)

            def send(step, carry, low=low):
                far_y = lax.rem(my_y + 2 + step // 2, lanes_x)
                peer = far_y * share + low * 2 + lax.rem(me + step, 2)
                leaving, landing = (group_of(peer), me) if which in (SIG, MID) else (peer, mine)
                remote(
                    out_buf.at[which, leaving], in_buf.at[which, landing], which, (row, peer)
                )
                return carry

            if apart:
                lax.fori_loop(0, share, send, 0)
            else:
                lax.fori_loop(0, share // 2, send, 0)
                lax.fori_loop(share // 2 + 1, share, send, 0)
        if which in (SIG, MID):
            in_buf[which, me] = out_buf[which, mine]
        else:
            in_buf[which, mine] = out_buf[which, me]

    def wait_for(sem, which, count):
        part = in_buf.at[0, pl.ds(0, count)]
        pltpu.make_async_copy(part, part, sem.at[which]).wait()

    def wait_either(sem, which, count, less):
        @pl.when(less)
        def _():
            wait_for(sem, which, count - 1)

        @pl.when(jnp.logical_not(less))
        def _():
            wait_for(sem, which, count)

    def line_up(part, block, blocks):
        part = part.astype(F32)
        for own in range(OWN):
            rows = part[:, own * UNITS : (own + 1) * UNITS, :].reshape(blocks * UNITS, LANES)
            lined[
                block * UNITS : (block + blocks) * UNITS, own * LANES : (own + 1) * LANES
            ] = rows.astype(BF16)

    def transform(spec):
        wide[...] = jnp.dot(first[...], lined[0:ROWS, :], preferred_element_type=F32)
        for own in range(OWN):
            lanes = slice(own * LANES, (own + 1) * LANES)
            rows = slice(own * ROWS, (own + 1) * ROWS)
            real, imag = wide[0:ROWS, lanes], wide[ROWS : 2 * ROWS, lanes]
            cos, sin = turn_cos[...], turn_sin[...]
            mixed[rows, 0:LANES] = (real * cos + imag * sin).astype(BF16)
            mixed[rows, LANES : 2 * LANES] = (imag * cos - real * sin).astype(BF16)
        spec[...] = jnp.dot(mixed[...], second[...], preferred_element_type=F32)

    def multiply(left, right, conjugate):
        for own in range(OWN):
            rows = slice(own * ROWS, (own + 1) * ROWS)
            left_re, left_im = left[rows, 0:LANES], left[rows, LANES : 2 * LANES]
            right_re, right_im = right[rows, 0:LANES], right[rows, LANES : 2 * LANES]
            if conjugate:
                real = left_re * right_re + left_im * right_im
                imag = left_re * right_im - left_im * right_re
            else:
                real = left_re * right_re - left_im * right_im
                imag = left_re * right_im + left_im * right_re
            mixed[rows, 0:LANES] = real.astype(BF16)
            mixed[rows, LANES : 2 * LANES] = imag.astype(BF16)

    def transform_back(which):
        for own in range(OWN):
            lanes = slice(own * LANES, (own + 1) * LANES)
            rows = slice(own * ROWS, (own + 1) * ROWS)
            both = jnp.dot(mixed[rows, :], second_t[...], preferred_element_type=F32)
            real, imag = both[:, 0:LANES], both[:, LANES : 2 * LANES]
            cos, sin = turn_cos[...], turn_sin[...]
            lined[0:ROWS, lanes] = (real * cos - imag * sin).astype(BF16)
            lined[ROWS : 2 * ROWS, lanes] = (real * sin + imag * cos).astype(BF16)
        values = jnp.dot(first_t[...], lined[...], preferred_element_type=F32) * SCALE
        parts = [
            values[:, own * LANES : (own + 1) * LANES].reshape(ctx_size, UNITS, LANES)
            for own in range(OWN)
        ]
        message = jnp.concatenate(parts, axis=1).astype(BF16)
        if which != GRF:
            out_buf[which] = message
            return
        for pair in range(ctx_size // 2):
            part_y, part_low = pair // (share // 2), pair % (share // 2)
            group = (part_y + part_low) % lanes_x
            out_part[group, 2 * part_y : 2 * part_y + 2] = message[2 * pair : 2 * pair + 2]

    diagonal = my_y + my_low
    filt_slot = 2 * my_y + lax.rem(me, 2)
    fetches_own = lax.rem(2 * diagonal, lanes_x) == my_x

    loads[0].wait()
    split_channels(FIL, lambda lanes: filt[:, lanes].astype(F32))
    pl.semaphore_wait(barrier, ctx_size - 1 + lanes_x)

    def send_filter(step, carry):
        far_y = lax.rem(my_y + 2 + step // 2, lanes_x)
        low = lax.rem(my_x + 3 * lanes_x - diagonal - far_y, lanes_x)
        peer = far_y * share + low * 2 + lax.rem(me + step, 2)

        @pl.when(peer != me)
        def _():
            leaving = out_buf.at[FIL, group_of(peer)]
            remote(leaving, in_filt.at[my_x, filt_slot], FIL, (row, peer))

        return carry

    lax.fori_loop(0, share, send_filter, 0)

    @pl.when(fetches_own)
    def _():
        in_filt[my_x, filt_slot] = out_buf[FIL, mine]

    loads[1].wait()
    split_channels(SIG, lambda lanes: signal[:, lanes].astype(F32))
    exchange(SIG)
    loads[2].wait()
    loads[3].wait()
    split_channels(MID, lambda lanes: gate[:, lanes].astype(F32) * cot[:, lanes].astype(F32))
    wait_either(recv_sem, FIL, share, fetches_own)
    for step in range(1, lanes_x):
        peer = lax.rem(my_x + step, lanes_x) * 2 + my_z
        remote(in_filt.at[my_x], in_filt.at[my_x], FIL_X, (peer, me))
    exchange(MID)

    for copy in loads[4:]:
        copy.wait()
    wait_for(recv_sem, SIG, ctx_size - 1)
    line_up(in_buf[SIG], 0, ctx_size)
    transform(spec_x)
    wait_for(recv_sem, FIL_X, share * (lanes_x - 1))
    for pair in range(ctx_size // 2):
        part_y, part_low = pair // (share // 2), pair % (share // 2)
        group = lax.rem(part_y + part_low + diagonal, lanes_x)
        line_up(in_filt[group, 2 * part_y : 2 * part_y + 2], 2 * pair, 2)
    transform(spec_h)
    multiply(spec_h, spec_x, False)
    transform_back(CNV)
    exchange(CNV)

    wait_for(recv_sem, MID, ctx_size - 1)
    line_up(in_buf[MID], 0, ctx_size)
    transform(spec_g)
    multiply(spec_x, spec_g, True)
    transform_back(GRF)
    for turn in range(lanes_x):
        part_y = lax.rem(my_y + 2 + turn, lanes_x)
        for step in range(1, lanes_x):
            peer = lax.rem(my_x + step, lanes_x)
            blocks = pl.ds(2 * part_y, 2)
            remote(
                out_part.at[peer, blocks],
                in_part.at[my_x, blocks],
                GRF_X + part_y,
                (peer * 2 + my_z, me),
            )
    in_part[my_x] = out_part[my_x]

    multiply(spec_h, spec_g, True)
    transform_back(GRS)
    exchange(GRS)

    to_row = mine // per_row
    slot = my_z * per_row + lax.rem(mine, per_row)
    stays = jnp.logical_and(to_row == row, lax.rem(diagonal, lanes_x) == my_x)

    def send_sums(part_y):
        wait_for(recv_sem, GRF_X + part_y, 2 * (lanes_x - 1))
        blocks = pl.ds(2 * part_y, 2)
        total = in_part[0, blocks].astype(F32)
        for part in range(1, lanes_x):
            total = total + in_part[part, blocks].astype(F32)
        out_sum[blocks] = total.astype(BF16)
        low = lax.rem(my_x + lanes_x - part_y, lanes_x)
        for core in range(2):
            block = 2 * part_y + core
            peer = part_y * share + low * 2 + core
            leaves = jnp.logical_or(to_row != row, peer != me)

            @pl.when(leaves)
            def _(block=block, peer=peer):
                remote(out_sum.at[block], in_sum.at[slot], GRF, (to_row, peer))

    for turn in range(lanes_x):
        send_sums(lax.rem(my_y + 2 + turn, lanes_x))

    @pl.when(stays)
    def _():
        in_sum[slot] = out_sum[filt_slot]

    wait_for(recv_sem, CNV, ctx_size - 1)
    stage[...] = in_buf[CNV].astype(F32).reshape(ctx_size * OWN * UNITS, LANES)
    for unit in range(UNITS):
        lanes = pl.ds(unit * LANES, LANES)
        conv = stage[pl.ds(unit, ctx_size * OWN, stride=UNITS), :]
        gated[:, lanes] = (gate[:, lanes].astype(F32) * conv).astype(BF16)
        grad_gate[:, lanes] = (cot[:, lanes].astype(F32) * conv).astype(BF16)

    wait_either(recv_sem, GRF, 2 * per_row, stays)
    total = in_sum[0:per_row].astype(F32) + in_sum[per_row : 2 * per_row].astype(F32)
    stage[0 : per_row * OWN * UNITS, :] = total.reshape(per_row * OWN * UNITS, LANES)
    for unit in range(UNITS):
        lanes = pl.ds(unit * LANES, LANES)
        grad_filter[:, lanes] = stage[pl.ds(unit, per_row * OWN, stride=UNITS), :].astype(BF16)

    wait_for(recv_sem, GRS, ctx_size - 1)
    stage[...] = in_buf[GRS].astype(F32).reshape(ctx_size * OWN * UNITS, LANES)
    for unit in range(UNITS):
        lanes = pl.ds(unit * LANES, LANES)
        grad_signal[:, lanes] = stage[pl.ds(unit, ctx_size * OWN, stride=UNITS), :].astype(BF16)

    for which in (SIG, MID, CNV, GRS):
        wait_for(send_sem, which, ctx_size - 1)
    wait_for(send_sem, FIL_X, share * (lanes_x - 1))
    for part_y in range(lanes_x):
        wait_for(send_sem, GRF_X + part_y, 2 * (lanes_x - 1))
    wait_either(send_sem, GRF, share, stays)
    wait_either(send_sem, FIL, share, fetches_own)


def hand_on(*refs):
    sources, targets, sem = refs[0:4], refs[4:8], refs[8]
    copies = [
        pltpu.make_async_copy(source, target, sem.at[index])
        for index, (source, target) in enumerate(zip(sources, targets))
    ]
    for copy in copies:
        copy.start()
    for copy in copies:
        copy.wait()


def per_device(signal, gate, filter_param, cotangent):
    ctx_size = lax.axis_size("ctx")
    dp_size = lax.axis_size("dp")
    channels, length = filter_param.shape
    lanes_x = dp_size // 2
    share = ctx_size // lanes_x
    block = (channels, length)
    part = (channels // dp_size, length)
    outer = pl.BlockSpec(memory_space=pltpu.HBM)
    inner = pl.BlockSpec(memory_space=pltpu.VMEM)
    message = (OWN * UNITS, LANES)
    spectrum = pltpu.VMEM((OWN * ROWS, 2 * LANES), F32)
    outs = pl.pallas_call(
        functools.partial(kernel, ctx_size, dp_size),
        out_shape=tuple(pltpu.VMEM(shape, BF16) for shape in (block, block, block, part)),
        in_specs=[outer] * 10,
        out_specs=(inner,) * 4,
        scratch_shapes=[
            pltpu.VMEM(block, BF16),
            pltpu.VMEM(block, BF16),
            pltpu.VMEM(block, BF16),
            pltpu.VMEM(block, BF16),
            pltpu.VMEM((2 * ROWS, ROWS), BF16),
            pltpu.VMEM((ROWS, 2 * ROWS), BF16),
            pltpu.VMEM((2 * LANES, 2 * LANES), BF16),
            pltpu.VMEM((2 * LANES, 2 * LANES), BF16),
            pltpu.VMEM((ROWS, LANES), F32),
            pltpu.VMEM((ROWS, LANES), F32),
            pltpu.VMEM((5, ctx_size) + message, BF16),
            pltpu.VMEM((4, ctx_size) + message, BF16),
            pltpu.VMEM((lanes_x, share) + message, BF16),
            pltpu.VMEM((lanes_x, share) + message, BF16),
            pltpu.VMEM((lanes_x, share) + message, BF16),
            pltpu.VMEM((share,) + message, BF16),
            pltpu.VMEM((2 * ctx_size // dp_size,) + message, BF16),
            pltpu.VMEM((ctx_size * OWN * UNITS, LANES), F32),
            pltpu.VMEM((2 * ROWS, OWN * LANES), F32),
            pltpu.VMEM((2 * ROWS, OWN * LANES), BF16),
            pltpu.VMEM((OWN * ROWS, 2 * LANES), BF16),
            spectrum,
            spectrum,
            spectrum,
            pltpu.SemaphoreType.DMA((7 + lanes_x,)),
            pltpu.SemaphoreType.DMA((7 + lanes_x,)),
            pltpu.SemaphoreType.DMA((10,)),
        ],
        compiler_params=pltpu.CompilerParams(
            collective_id=0, has_side_effects=True, vmem_limit_bytes=60 * 1024 * 1024
        ),
    )(
        signal.reshape(block),
        gate.reshape(block),
        filter_param,
        cotangent.reshape(block),
        *tables(),
    )
    outs = pl.pallas_call(
        hand_on,
        out_shape=tuple(jax.ShapeDtypeStruct(shape, BF16) for shape in (block, block, block, part)),
        in_specs=[inner] * 4,
        out_specs=(outer,) * 4,
        scratch_shapes=[pltpu.SemaphoreType.DMA((4,))],
        compiler_params=pltpu.CompilerParams(vmem_limit_bytes=4 * 1024 * 1024),
    )(*outs)
    return (outs[0][None], outs[1][None], outs[2][None], outs[3])


def solution(mesh):
    in_specs = (P("dp", None, "ctx"), P("dp", None, "ctx"), P(None, "ctx"), P("dp", None, "ctx"))
    out_specs = (P("dp", None, "ctx"), P("dp", None, "ctx"), P("dp", None, "ctx"), P("dp", "ctx"))
    return jax.shard_map(
        per_device, mesh=mesh, in_specs=in_specs, out_specs=out_specs, check_vma=False
    )
```
